256 devices in a mesh: ma: 64 (over z, y, core), ta: 4 (over x).
Axes of the slice: x: 4, y: 4, z: 8, core: 2. Of those that a mesh axis runs over, the one named last changes fastest.
Arguments:
- harmonics: float32 [4, 2, 64, 2, 8192], P('ta', None, 'ma'), may hold values from -0.01953125 to 0.01953125
- noise_weight: float32 [4, 64, 16384], P('ta', 'ma'), may hold values from 0.3 to 3
- order_table: int32 [64], replicated, may hold values from 0 to 8191, as said below
- curve_weight: float32 [2, 32], replicated, may hold values from -6 to 6
Outputs:
- kappa_map: float32 [4, 2, 64, 16384], P('ta', None, 'ma')
- euler_curve: float32 [2, 32], replicated
- alm_grad: float32 [4, 2, 64, 2, 8192], P('ta', None, 'ma')
The draws below stay inside these ranges and needn't reach their ends.
Inputs may be any that keep to these rules, and one draw needn't show every extreme that they name: `order_table`: each interval of 128 orders that starts at a multiple of 128 holds exactly one entry; the 1 entries of each aligned run (the rows of one device) lie in 1 consecutive such intervals, in increasing order, the first of which has an index that is a multiple of 1.
All inputs are finite; a program needn't handle non-finite values.
Results may differ from the reference program's by a relative error of at most 0.0003.
Values sent between devices are 32-bit elements; how exact they have to be, the bound alone decides.
No kernel may reach another device: no remote copies, remote signals or barrier semaphores. Data moves between devices by JAX's collectives and lax.ppermute only.
A program may use at most 128 MiB of HBM per device.

```python
import math
import jax
import jax.numpy as jnp
from jax import lax

NPIX = 16384
LMAX = 8192
THRESH = 32
REALS = 2
M_DEV = 1
BINS = 4
M_TOTAL = 64
MSTEP = 128
R_TOTAL = 64


def draw_order_table(key, part):
    block_total = M_TOTAL // M_DEV
    shuffle_key = jax.random.fold_in(key, 11)
    offset_key = jax.random.fold_in(key, 12)
    shuffled = jax.random.permutation(shuffle_key, block_total)
    bands = (shuffled[:, None] * M_DEV + jnp.arange(M_DEV)[None, :]).reshape(M_TOTAL).astype(jnp.int32)
    if MSTEP >= 2:
        raw_offset = jax.random.randint(offset_key, (M_TOTAL,), 0, MSTEP // 2).astype(jnp.int32)
        offsets = 2 * raw_offset + bands % 2
        offsets = jnp.where(bands == 0, 0, offsets)
        offsets = jnp.where(bands == M_TOTAL - 1, MSTEP - 1, offsets)
    else:
        offsets = jnp.zeros((M_TOTAL,), jnp.int32)
    return (bands * MSTEP + offsets).astype(jnp.int32)


def steps_of(rng, dims, pieces, least, top_value):
    def one(dim, parts):
        steps = jax.random.uniform(jax.random.fold_in(jax.random.fold_in(rng, 6), dim), (parts,), jnp.float32, least / len(pieces), top_value / len(pieces))
        return jnp.repeat(jnp.exp(steps), dims[dim] // parts).reshape((-1,) + (1,) * (len(dims) - dim - 1))

    factor_of = one(*pieces[0])
    for cut in pieces[1:]:
        factor_of = factor_of * one(*cut)
    return factor_of


def gaussian(stream_key, extent, width, bound, pieces=(), held_as=jnp.bfloat16):
    values = jax.random.normal(stream_key, extent, jnp.float32) * width
    if len(pieces) > 0:
        values = steps_of(stream_key, extent, pieces, -0.22, 0.18) * values
    return jnp.clip(values, min=-bound, max=bound).astype(held_as)


def setup_inputs(seed: int = 0) -> dict:
    key_of = jax.random.split(jax.random.key(seed), 5)
    return {
        "harmonics": gaussian(key_of[0], (BINS, REALS, M_TOTAL, 2, LMAX), (M_TOTAL * LMAX // 6) ** -0.5, 0.01953125, ((0, 4), (2, 64)), jnp.float32),
        "noise_weight": jnp.clip(jnp.exp(math.log(3.0) - 2.3025851 * jax.random.uniform(key_of[1], (BINS, R_TOTAL, NPIX), jnp.float32) ** steps_of(key_of[1], (BINS, R_TOTAL, NPIX), ((0, 4), (1, 64)), -0.2, 0.2)), 0.3, 3.0),
        "order_table": draw_order_table(jax.random.fold_in(key_of[4], 71), 0),
        "curve_weight": gaussian(key_of[3], (REALS, THRESH), 1.0, 6.0, (), jnp.float32),
    }


SOFTNESS = 0.25
HIGHEST = lax.Precision.HIGHEST

def cycle_geometry(cycle_ids, total_cycles, pixel_count):
    heights = 4.0 * (total_cycles - 2.0 * cycle_ids.astype(jnp.float32)) / (3.0 * pixel_count)
    parity = (cycle_ids + 1 + pixel_count // 4 - total_cycles // 2) % 2
    return (heights, parity)

def start_value(order_value, heights):
    return jnp.exp(0.5 * jnp.log((2.0 * order_value + 1.0) / (4.0 * math.pi)) - 0.25 * jnp.log(math.pi * (order_value + 0.25)) + 0.5 * order_value * jnp.log(1.0 - heights * heights))

def transfer_matrix(order_value, offsets, heights):
    degree = order_value + offsets
    alpha_term = jnp.sqrt(jnp.maximum((2.0 * degree - 1.0) * (2.0 * degree + 1.0), 0.0) / jnp.maximum(offsets * (offsets + 2.0 * order_value), 1.0))
    beta_term = jnp.sqrt(jnp.maximum((offsets - 1.0) * (offsets - 1.0 + 2.0 * order_value), 0.0) / jnp.maximum((2.0 * degree - 3.0) * (2.0 * degree - 1.0), 1.0))
    moving = offsets > 0.5
    upper_left = jnp.where(moving, alpha_term * heights, 1.0)
    upper_right = jnp.where(moving, -alpha_term * beta_term, 0.0)
    lower_left = jnp.where(moving, 1.0, 0.0)
    lower_right = jnp.where(moving, 0.0, 1.0)
    return (upper_left, upper_right, lower_left, lower_right)

def legendre_table(order_number, heights, degree_count):
    order_value = order_number.astype(jnp.float32)
    seed_value = start_value(order_value, heights)

    def advance(loop_state, offset_value):
        current, previous = loop_state
        matrix = transfer_matrix(order_value, offset_value, heights)
        following = matrix[0] * current + matrix[1] * previous
        return ((following, current), following)
    _, later_rows = lax.scan(advance, (seed_value, jnp.zeros_like(seed_value)), jnp.arange(1, degree_count).astype(jnp.float32))
    return jnp.concatenate([seed_value[None], later_rows], axis=0)

def rooted_counts(cycle_stack, levels, parity, inside):
    level_shape = (levels.shape[0],) + (1,) * cycle_stack.ndim
    indicator = jax.nn.sigmoid((cycle_stack[None] - levels.reshape(level_shape)) / SOFTNESS)
    upper_rows = indicator[..., :-1, :]
    lower_rows = indicator[..., 1:, :]
    east_side = jnp.roll(upper_rows, -1, axis=-1)
    lower_left = jnp.where(parity[:, None] == 1, lower_rows, jnp.roll(lower_rows, 1, axis=-1))
    lower_right = jnp.roll(lower_left, -1, axis=-1)
    cell_terms = upper_rows * (1.0 - east_side) + inside[:, None] * upper_rows * (east_side * lower_right - lower_left - lower_right + lower_left * lower_right)
    return lax.optimization_barrier(jnp.sum(cell_terms, axis=-1))

def reference(harmonics, noise_weight, order_table, curve_weight):
    bin_count, realizations, total_orders, _, degree_count = harmonics.shape
    total_cycles = noise_weight.shape[1]
    pixel_count = noise_weight.shape[2]
    level_count = curve_weight.shape[1]
    orders = order_table.astype(jnp.int32)
    cycle_ids = jnp.arange(total_cycles).astype(jnp.int32)
    heights, parity = cycle_geometry(cycle_ids, total_cycles, pixel_count)
    field_rows = bin_count * realizations * 2
    rows_first = jnp.moveaxis(harmonics, 2, 0).reshape(total_orders, field_rows, degree_count)
    degree_ids = jnp.arange(degree_count).astype(jnp.int32)

    def synthesize(packed):
        order_number, coefficients = packed
        legendre = legendre_table(order_number, heights, degree_count)
        inside = (degree_ids < degree_count - order_number).astype(jnp.float32)
        return jnp.dot(coefficients * inside, legendre, precision=HIGHEST, preferred_element_type=jnp.float32)
    spectra = lax.map(synthesize, (orders, rows_first)).reshape(total_orders, bin_count, realizations, 2, total_cycles)
    order_weight = jnp.where(orders == 0, 1.0, 2.0).astype(jnp.float32)
    pixels = jnp.arange(pixel_count).astype(jnp.int32)

    def cycle_phases(cycle_number):
        phases = (orders[:, None] * (2 * pixels[None, :] + parity[cycle_number]) % (2 * pixel_count)).astype(jnp.float32) * (math.pi / pixel_count)
        return (jnp.cos(phases), jnp.sin(phases))

    def cycle_map(cycle_number):
        cosine, sine = cycle_phases(cycle_number)
        real_part = spectra[:, :, :, 0, cycle_number] * order_weight[:, None, None]
        imag_part = spectra[:, :, :, 1, cycle_number] * order_weight[:, None, None]
        return jnp.einsum('mbr,mp->brp', real_part, cosine, precision=HIGHEST) - jnp.einsum('mbr,mp->brp', imag_part, sine, precision=HIGHEST)
    kappa_map = jnp.transpose(lax.map(cycle_map, cycle_ids), (1, 2, 0, 3))
    signal_ratio = kappa_map * noise_weight[:, None]
    padded = jnp.concatenate([signal_ratio, jnp.zeros_like(signal_ratio[:, :, :1])], axis=2)
    inside_cycles = (cycle_ids < total_cycles - 1).astype(jnp.float32)
    levels = -3.0 + 6.0 * jnp.arange(level_count).astype(jnp.float32) / (level_count - 1)
    level_weights = curve_weight / math.sqrt(total_cycles * pixel_count)

    def per_bin(bin_stack):

        def level_step(level_number, loop_state):
            counts, accumulated = loop_state
            level_slice = lax.dynamic_slice_in_dim(levels, level_number, 1)

            def counting(stack_value):
                return rooted_counts(stack_value, level_slice, parity, inside_cycles)
            counted, pullback = jax.vjp(counting, bin_stack)
            cotangent = jnp.broadcast_to(lax.dynamic_slice_in_dim(level_weights, level_number, 1, 1).T[:, :, None], counted.shape)
            accumulated = accumulated + pullback(cotangent)[0]
            counts = counts.at[:, level_number].set(lax.optimization_barrier(jnp.sum(counted[0], axis=-1)))
            return (counts, accumulated)
        initial = (jnp.zeros((realizations, level_count), jnp.float32), jnp.zeros_like(bin_stack))
        return lax.fori_loop(0, level_count, level_step, initial)
    counts, stack_grad = lax.map(per_bin, padded)
    euler_curve = lax.optimization_barrier(jnp.sum(counts, axis=0)) / (bin_count * total_cycles * pixel_count)
    kappa_grad = stack_grad[:, :, :total_cycles] * noise_weight[:, None]

    def cycle_dual(cycle_number):
        cosine, sine = cycle_phases(cycle_number)
        cycle_grad = kappa_grad[:, :, cycle_number, :]
        cos_sum = jnp.einsum('brp,mp->mbr', cycle_grad, cosine, precision=HIGHEST)
        sin_sum = jnp.einsum('brp,mp->mbr', cycle_grad, sine, precision=HIGHEST)
        return jnp.stack([order_weight[:, None, None] * cos_sum, -order_weight[:, None, None] * sin_sum], axis=-1)
    spectra_grad = jnp.transpose(lax.map(cycle_dual, cycle_ids), (1, 2, 3, 4, 0)).reshape(total_orders, field_rows, total_cycles)

    def adjoint(packed):
        order_number, dual_rows = packed
        legendre = legendre_table(order_number, heights, degree_count)
        inside = (degree_ids < degree_count - order_number).astype(jnp.float32)
        return jnp.dot(dual_rows, legendre.T, precision=HIGHEST, preferred_element_type=jnp.float32) * inside
    harmonic_grad = lax.map(adjoint, (orders, spectra_grad)).reshape(total_orders, bin_count, realizations, 2, degree_count)
    alm_grad = jnp.moveaxis(harmonic_grad, 0, 2)
    return (kappa_map, euler_curve, alm_grad)
```

```python
import math

import jax
import jax.numpy as jnp
from jax import lax
from jax.experimental import pallas as pl
from jax.experimental.pallas import tpu as pltpu
from jax.sharding import PartitionSpec as P

F32 = jnp.float32
HIGHEST = lax.Precision.HIGHEST
NPIX = 16384
LMAX = 8192
CYCLES = 64
LEVELS = 32
SIDE = 128
ROWS = 24
FAR = -1.0e9


def iota(shape, dim):
    return lax.broadcasted_iota(jnp.int32, shape, dim)


def dot(a, b, contract):
    return lax.dot_general(a, b, ((contract[:1], contract[1:]), ((), ())), precision=HIGHEST,
                           preferred_element_type=F32)


def slot_cycle(half, row):
    own = jnp.where(row < 16, row + 16 * half, -1)
    return jnp.where((row == 16) & (half == 0), 32, own)


def selector():
    shape = (CYCLES, 4 * ROWS)
    cycle, column = iota(shape, 0), iota(shape, 1)
    odd = (column >= 2 * ROWS).astype(jnp.int32)
    rest = column - 2 * ROWS * odd
    half = (rest >= ROWS).astype(jnp.int32)
    held = slot_cycle(half, rest - ROWS * half)
    mirrored = jnp.where(cycle > 32, 64 - cycle, cycle)
    sign = jnp.where((cycle > 32) & (odd == 1), -1.0, 1.0)
    return jnp.where(held == mirrored, sign, 0.0).astype(F32)


def turn_cos_sin(index, whole):
    quarter = whole // 4
    index = index & (whole - 1)
    quadrant = (index + quarter // 2) >> (quarter.bit_length() - 1)
    x = (index - quadrant * quarter).astype(F32) * (2.0 * math.pi / whole)
    y = x * x
    sine = x * (1.0 + y * (-1.0 / 6 + y * (1.0 / 120 + y * (-1.0 / 5040 + y * (1.0 / 362880)))))
    cosine = 1.0 + y * (-0.5 + y * (1.0 / 24 + y * (-1.0 / 720 + y * (1.0 / 40320 - y * (1.0 / 3628800)))))
    swap = (quadrant & 1) == 1
    c = jnp.where(swap, sine, cosine)
    s = jnp.where(swap, cosine, sine)
    c = jnp.where(((quadrant + 1) & 2) == 2, -c, c)
    s = jnp.where((quadrant & 2) == 2, -s, s)
    return c, s


def legendre_kernel(orders, harmonics, table, sent, first, second, coefficients):
    ma = lax.axis_index("ma")
    order = orders[ma]
    order_value = order.astype(F32)
    square = (SIDE, SIDE)
    lane, step = iota(square, 1), iota(square, 0)
    degree_index = (lane >> 1) * SIDE + step
    j = degree_index.astype(F32)
    degree = order_value + j
    alpha = jnp.sqrt(
        jnp.maximum((2.0 * degree - 1.0) * (2.0 * degree + 1.0), 0.0)
        / jnp.maximum(j * (j + 2.0 * order_value), 1.0)
    )
    beta = jnp.sqrt(
        jnp.maximum((j - 1.0) * (j - 1.0 + 2.0 * order_value), 0.0)
        / jnp.maximum((2.0 * degree - 3.0) * (2.0 * degree - 1.0), 1.0)
    )
    moving = degree_index > 0
    first[...] = jnp.where(moving, alpha, 0.0)
    second[...] = jnp.where(moving, -alpha * beta, 1.0)
    valid = degree_index < LMAX - order
    even_lane = (lane & 1) == 0
    for r in range(2):
        turned = harmonics[r].T
        real = jnp.where(even_lane, turned, pltpu.roll(turned, 1, 1))
        imag = jnp.where(even_lane, pltpu.roll(turned, SIDE - 1, 1), turned)
        coefficients[2 * r] = jnp.where(valid, real, 0.0)
        coefficients[2 * r + 1] = jnp.where(valid, imag, 0.0)

    shape = (ROWS, SIDE)
    row, half = iota(shape, 0), iota(shape, 1) & 1
    held = slot_cycle(half, row)
    z = jnp.where(held >= 0, 4.0 * (64.0 - 2.0 * held.astype(F32)) / (3.0 * NPIX), 0.0)
    below_one = 1.0 - (1.0 - z * z)
    log_term = -below_one * (1.0 + below_one * (0.5 + below_one * (1.0 / 3.0)))
    full = jnp.full(shape, order_value, F32)
    seed = jnp.exp(
        0.5 * jnp.log((2.0 * full + 1.0) / (4.0 * math.pi))
        - 0.25 * jnp.log(math.pi * (full + 0.25))
        + 0.5 * full * log_term
    )

    unroll = 8

    def compose(block, state):
        pu, pl_, qu, ql = state
        for s in range(unroll):
            i = block * unroll + s
            zc = z * first[pl.ds(i, 1), :]
            c2 = second[pl.ds(i, 1), :]
            pu, pl_ = zc * pu + c2 * pl_, pu
            qu, ql = zc * qu + c2 * ql, qu
        return pu, pl_, qu, ql

    ones, zeros = jnp.ones(shape, F32), jnp.zeros(shape, F32)
    a, c, b, d = lax.fori_loop(0, SIDE // unroll, compose, (ones, zeros, zeros, ones))
    lanes = iota(shape, 1)
    for by in (2, 4, 8, 16, 32, 64):
        inside = lanes >= by
        ea = jnp.where(inside, pltpu.roll(a, by, 1), 1.0)
        eb = jnp.where(inside, pltpu.roll(b, by, 1), 0.0)
        ec = jnp.where(inside, pltpu.roll(c, by, 1), 0.0)
        ed = jnp.where(inside, pltpu.roll(d, by, 1), 1.0)
        a, b, c, d = a * ea + b * ec, a * eb + b * ed, c * ea + d * ec, c * eb + d * ed
    started = lanes >= 2
    upper = jnp.where(started, pltpu.roll(b, 2, 1) * seed, 0.0)
    lower = jnp.where(started, pltpu.roll(d, 2, 1) * seed, seed)

    def advance(block, state):
        upper, lower, sums = state[0], state[1], list(state[2:])
        for s in range(unroll):
            i = block * unroll + s
            zc = z * first[pl.ds(i, 1), :]
            upper, lower = zc * upper + second[pl.ds(i, 1), :] * lower, upper
            table[i] = upper
            for f in range(4):
                at = 4 * (s % 2) + f
                sums[at] = sums[at] + coefficients[f, pl.ds(i, 1), :] * upper
        return (upper, lower, *sums)

    state = lax.fori_loop(0, SIDE // unroll, advance, (upper, lower) + (zeros,) * 8)
    sums = state[2:]
    pieces = []
    for parity in range(2):
        for which in range(2):
            total = None
            for f in range(4):
                pick = ((iota(square, 0) & 1) == which) & (iota(square, 1) == f)
                part = dot(sums[4 * parity + f], pick.astype(F32), (1, 0))
                total = part if total is None else total + part
            pieces.append(total)
    stacked = jnp.concatenate(pieces, axis=0)
    own = dot(selector(), stacked, (1, 0))
    before = pltpu.roll(own, 1, 0)
    after = pltpu.roll(own, CYCLES - 1, 0)
    sent[...] = own + pltpu.roll(before, 4, 1) + pltpu.roll(after, 8, 1)


def neighbour(x, by):
    lane = iota((SIDE, SIDE), 1)
    if by == 1:
        moved = pltpu.roll(x, SIDE - 1, 1)
        return jnp.where(lane == SIDE - 1, pltpu.roll(moved, SIDE - 1, 0), moved)
    moved = pltpu.roll(x, 1, 1)
    return jnp.where(lane == 0, pltpu.roll(moved, 1, 0), moved)


def euler_kernel(orders_row, level_weights, received, noise, noise_before, noise_after, kappa, sent,
                 fields, counts):
    cycle = lax.axis_index("ma")
    parity = (cycle + 1 + NPIX // 4 - CYCLES // 2) % 2
    square = (SIDE, SIDE)
    lane, row = iota(square, 1), iota(square, 0)
    order = jnp.concatenate([orders_row[...], orders_row[...]], axis=1)
    orders = jnp.broadcast_to(order, square)
    a_cos, a_sin = turn_cos_sin(orders * row, SIDE)
    orders_down = orders.astype(F32).T.astype(jnp.int32)
    b_cos, b_sin = turn_cos_sin(orders_down * lane, NPIX)
    basis = jnp.where(row < CYCLES, b_cos, b_sin)
    spin_cos, spin_sin = turn_cos_sin(jnp.broadcast_to(order, (8, SIDE)), 2 * NPIX)
    spin_cos, spin_sin = spin_cos[:1], spin_sin[:1]
    weight = jnp.where(order == 0, 1.0, 2.0)
    low = iota((1, SIDE), 1) < CYCLES

    flipped = jnp.concatenate([received[...], received[...]], axis=0).T
    lefts = []
    for kk in range(3):
        turned = parity == 1 if kk == 0 else parity == 0
        cs = jnp.where(turned, spin_cos, 1.0)
        sn = jnp.where(turned, spin_sin, 0.0)
        for r in range(2):
            real = flipped[4 * kk + 2 * r : 4 * kk + 2 * r + 1]
            imag = flipped[4 * kk + 2 * r + 1 : 4 * kk + 2 * r + 2]
            c_real = weight * (real * cs - imag * sn)
            c_imag = weight * (real * sn + imag * cs)
            u = jnp.where(low, c_real, -c_imag)
            v = jnp.where(low, -c_imag, -c_real)
            lefts.append(u * a_cos + v * a_sin)
    maps = dot(jnp.concatenate(lefts, axis=0), basis, (1, 0))

    def ratio(kk, r, weights):
        return 2.0 * (maps[(2 * kk + r) * SIDE : (2 * kk + r + 1) * SIDE] * weights)

    for r in range(2):
        kappa[r] = maps[r * SIDE : (r + 1) * SIDE]
        here = ratio(0, r, noise[...])
        above = jnp.where(cycle > 0, ratio(1, r, noise_before[...]), FAR)
        below = jnp.where(cycle < CYCLES - 1, ratio(2, r, noise_after[...]), FAR)
        odd = parity == 1
        fields[r, 0] = here
        fields[r, 1] = neighbour(here, 1)
        fields[r, 2] = neighbour(here, -1)
        fields[r, 3] = jnp.where(odd, below, neighbour(below, -1))
        fields[r, 4] = jnp.where(odd, neighbour(below, 1), below)
        fields[r, 5] = jnp.where(odd, above, neighbour(above, -1))
        fields[r, 6] = jnp.where(odd, neighbour(above, 1), above)

    counts[...] = jnp.zeros_like(counts)
    for r in range(2):

        def tile(index, carry, r=r):
            at = pl.ds(pl.multiple_of(index * 8, 8), 8)
            held = [fields[r, n, at, :] for n in range(7)]
            total = jnp.zeros((8, SIDE), F32)
            for t in range(LEVELS):
                twice = 2.0 * (-3.0 + 6.0 * t / (LEVELS - 1))
                u, e, w, d, dd, n1, n2 = [jnp.tanh(x - twice) for x in held]
                inner = e * (dd + n2) + w * (d + n1) + d * dd + n1 * n2 - 2.0
                total = total + (level_weights[r, t] * inner) * (1.0 - u * u)
                counts[r * LEVELS + t] += (1.0 + u) * (1.0 - dd) * (d + e)
            fields[r, 0, at, :] = total
            return carry

        lax.fori_loop(0, SIDE // 8, tile, 0)

    scale = 1.0 / (4.0 * math.sqrt(CYCLES * NPIX))
    duals = []
    for r in range(2):
        gradient = fields[r, 0] * (noise[...] * scale)
        sums = dot(gradient, basis, (1, 1))
        near = jnp.sum(sums * a_cos, axis=0, keepdims=True)
        far = jnp.sum(sums * a_sin, axis=0, keepdims=True)
        far = pltpu.roll(jnp.broadcast_to(far, (8, SIDE)), CYCLES, 1)[:1]
        both = near + jnp.where(low, -far, far)
        other = pltpu.roll(jnp.broadcast_to(both, (8, SIDE)), CYCLES, 1)[:1]
        cs = jnp.where(parity == 1, spin_cos, 1.0)
        sn = jnp.where(parity == 1, spin_sin, 0.0)
        duals.append(
            weight * jnp.where(low, both * cs - other * sn, -(both * cs + other * sn))
        )
    stacked = jnp.where(row == 0, duals[0], jnp.where(row == 1, duals[1], 0.0)).T
    per_order = stacked[:CYCLES] + pltpu.roll(stacked[CYCLES:], 2, 1)
    level_sums = jnp.sum(counts[...], axis=1) * -0.125
    padded = jnp.concatenate([jnp.zeros_like(level_sums), level_sums], axis=0)
    level_row = dot(jnp.ones((8, SIDE), F32), padded, (1, 1))[:1]
    sent[...] = per_order + level_row


def adjoint_kernel(orders, received, table, gradient, turned):
    order = orders[lax.axis_index("ma")]
    square = (SIDE, SIDE)
    lane, row = iota(square, 1), iota(square, 0)
    duals = dot(selector(), received[...], (0, 0))
    even = (iota((ROWS, SIDE), 1) & 1) == 0

    def column(parity, half, r, c):
        start = (2 * parity + half) * ROWS
        at = 2 * c + r
        return jnp.broadcast_to(duals[start : start + ROWS, at : at + 1], (ROWS, SIDE))

    factors = [
        [
            (
                jnp.where(even, column(parity, 0, r, 0), column(parity, 1, r, 1)),
                jnp.where(even, column(parity, 0, r, 1), column(parity, 1, r, 0)),
            )
            for r in range(2)
        ]
        for parity in range(2)
    ]

    def block(index, carry):
        rows = [[[], []], [[], []]]
        for s in range(8):
            values = table[index * 8 + s]
            for r in range(2):
                for kind in range(2):
                    product = values * factors[s % 2][r][kind]
                    rows[r][kind].append(jnp.sum(product, axis=0, keepdims=True))
        at = pl.ds(pl.multiple_of(index * 8, 8), 8)
        for r in range(2):
            straight = jnp.concatenate(rows[r][0], axis=0)
            crossed = jnp.concatenate(rows[r][1], axis=0)
            even_lane = (iota((8, SIDE), 1) & 1) == 0
            crossed = jnp.where(even_lane, pltpu.roll(crossed, SIDE - 1, 1), pltpu.roll(crossed, 1, 1))
            turned[r, at, :] = straight + crossed
        return carry

    lax.fori_loop(0, SIDE // 8, block, 0)
    for r in range(2):
        degree_index = (row >> 1) * SIDE + lane
        gradient[r] = jnp.where(degree_index < LMAX - order, turned[r].T, 0.0)


VMEM = pl.BlockSpec(memory_space=pltpu.VMEM)
SMEM = pl.BlockSpec(memory_space=pltpu.SMEM)
PARAMS = pltpu.CompilerParams(vmem_limit_bytes=40 * 1024 * 1024)


def shards(harmonics, noise_weight, order_table, curve_weight):
    ta_count = lax.axis_size("ta")
    ma_count = lax.axis_size("ma")
    noise = noise_weight.reshape(SIDE, SIDE)
    noise_before = lax.ppermute(noise, "ma", [(i, i + 1) for i in range(ma_count - 1)])
    noise_after = lax.ppermute(noise, "ma", [(i + 1, i) for i in range(ma_count - 1)])
    packed = harmonics.reshape(2, 2, 64, SIDE).transpose(0, 2, 1, 3).reshape(2, SIDE, SIDE)
    square = jax.ShapeDtypeStruct((CYCLES, SIDE), F32)
    table, sent = pl.pallas_call(
        legendre_kernel,
        in_specs=[SMEM, VMEM],
        out_specs=[VMEM, VMEM],
        out_shape=[jax.ShapeDtypeStruct((SIDE, ROWS, SIDE), F32), square],
        scratch_shapes=[
            pltpu.VMEM((SIDE, SIDE), F32),
            pltpu.VMEM((SIDE, SIDE), F32),
            pltpu.VMEM((4, SIDE, SIDE), F32),
        ],
        compiler_params=PARAMS,
        name="legendre",
    )(order_table, packed)
    received = lax.all_to_all(sent, "ma", split_axis=0, concat_axis=0, tiled=True)
    kappa, sent = pl.pallas_call(
        euler_kernel,
        in_specs=[VMEM, SMEM, VMEM, VMEM, VMEM, VMEM],
        out_specs=[VMEM, VMEM],
        out_shape=[jax.ShapeDtypeStruct((2, SIDE, SIDE), F32), square],
        scratch_shapes=[
            pltpu.VMEM((2, 7, SIDE, SIDE), F32),
            pltpu.VMEM((2 * LEVELS, 8, SIDE), F32),
        ],
        compiler_params=PARAMS,
        name="euler",
    )(order_table.reshape(1, CYCLES), curve_weight, received, noise, noise_before, noise_after)
    received = lax.all_to_all(sent, "ma", split_axis=0, concat_axis=0, tiled=True)
    counts = jnp.sum(received[:, CYCLES:], axis=0).reshape(2, LEVELS)
    one, two, three = [lax.ppermute(counts, "ta", [(i, i ^ by) for i in range(ta_count)]) for by in (1, 2, 3)]
    curve = ((counts + one) + (two + three)) / (ta_count * CYCLES * NPIX)
    gradient = pl.pallas_call(
        adjoint_kernel,
        in_specs=[SMEM, VMEM, VMEM],
        out_specs=VMEM,
        out_shape=jax.ShapeDtypeStruct((2, SIDE, SIDE), F32),
        scratch_shapes=[pltpu.VMEM((2, SIDE, SIDE), F32)],
        compiler_params=PARAMS,
        name="adjoint",
    )(order_table, received, table)
    gradient = gradient.reshape(2, 64, 2, SIDE).transpose(0, 2, 1, 3).reshape(1, 2, 1, 2, LMAX)
    return kappa.reshape(1, 2, 1, NPIX), curve, gradient


def solution(mesh):
    in_specs = (P("ta", None, "ma", None, None), P("ta", "ma", None), P(), P())
    out_specs = (P("ta", None, "ma", None), P(), P("ta", None, "ma", None, None))
    return jax.shard_map(shards, mesh=mesh, in_specs=in_specs, out_specs=out_specs, check_vma=False)
```

```python
import math

import jax
import jax.numpy as jnp
from jax import lax
from jax.experimental import pallas as pl
from jax.experimental.pallas import tpu as pltpu
from jax.sharding import PartitionSpec as P

F32 = jnp.float32
BF16 = jnp.bfloat16
HIGHEST = lax.Precision.HIGHEST
NPIX = 16384
LMAX = 8192
CYCLES = 64
LEVELS = 32
SIDE = 128
ROWS = 24
TILE = 16
FAR = -1.0e9


def iota(shape, dim):
    return lax.broadcasted_iota(jnp.int32, shape, dim)


def dot(a, b, contract):
    return lax.dot_general(a, b, ((contract[:1], contract[1:]), ((), ())), precision=HIGHEST,
                           preferred_element_type=F32)


def slot_cycle(half, row):
    own = jnp.where(row < 16, row + 16 * half, -1)
    return jnp.where((row == 16) & (half == 0), 32, own)


def selection(cycle, odd, half, row):
    mirrored = jnp.where(cycle > 32, 64 - cycle, cycle)
    sign = jnp.where((cycle > 32) & odd, -1.0, 1.0)
    return jnp.where(slot_cycle(half, row) == mirrored, sign, 0.0).astype(F32)


def split(x):
    high = x.astype(BF16)
    return high, (x - high.astype(F32)).astype(BF16)


def mxu(a, b):
    return lax.dot_general(a, b, (((1,), (0,)), ((), ())), preferred_element_type=F32)


def turn_cos_sin(index, whole):
    quarter = whole // 4
    index = index & (whole - 1)
    quadrant = (index + quarter // 2) >> (quarter.bit_length() - 1)
    x = (index - quadrant * quarter).astype(F32) * (2.0 * math.pi / whole)
    y = x * x
    sine = x * (1.0 + y * (-1.0 / 6 + y * (1.0 / 120 + y * (-1.0 / 5040 + y * (1.0 / 362880)))))
    cosine = 1.0 + y * (-0.5 + y * (1.0 / 24 + y * (-1.0 / 720 + y * (1.0 / 40320 - y * (1.0 / 3628800)))))
    swap = (quadrant & 1) == 1
    c = jnp.where(swap, sine, cosine)
    s = jnp.where(swap, cosine, sine)
    c = jnp.where(((quadrant + 1) & 2) == 2, -c, c)
    s = jnp.where((quadrant & 2) == 2, -s, s)
    return c, s


def make_basis(orders_row, turns, basis, basis_turned, small):
    square = (SIDE, SIDE)
    lane, row = iota(square, 1), iota(square, 0)
    twice = (iota((CYCLES, SIDE), 1) >> 1) == iota((CYCLES, SIDE), 0)
    eight = jnp.broadcast_to(orders_row[...].astype(F32), (8, CYCLES))
    eight = dot(eight, twice.astype(F32), (1, 0)).astype(jnp.int32)
    orders = jnp.broadcast_to(eight[:1], square)
    turns[0], turns[1] = turn_cos_sin(orders * row, SIDE)
    cosine, sine = turn_cos_sin(orders * row, NPIX)
    turned = jnp.where((lane & 1) == 0, cosine, sine)
    for ref, value in ((basis, turned.T), (basis_turned, turned)):
        ref[:, :SIDE], ref[:, SIDE:] = split(value)
    small[0], small[1] = turn_cos_sin(eight, 2 * NPIX)
    small[2] = jnp.where(eight == 0, 1.0, 2.0)


def legendre_kernel(orders_in, row_in, harmonics_in, table, sent, order_out, turns, basis, basis_turned, small_out,
                    first, second, coefficients, orders, harmonics, orders_row, sems):
    ma = lax.axis_index("ma")
    fetch_orders = pltpu.make_async_copy(orders_in, orders, sems.at[0])
    fetch_harmonics = pltpu.make_async_copy(harmonics_in, harmonics, sems.at[1])
    fetch_row = pltpu.make_async_copy(row_in, orders_row, sems.at[2])
    fetch_orders.start()
    fetch_row.start()
    fetch_harmonics.start()
    fetch_orders.wait()
    order = orders[ma]
    order_out[...] = jnp.full(order_out.shape, order, jnp.int32)
    order_value = order.astype(F32)
    square = (SIDE, SIDE)
    lane, step = iota(square, 1), iota(square, 0)
    degree_index = (lane >> 1) * SIDE + step
    j = degree_index.astype(F32)
    degree = order_value + j
    alpha = jnp.sqrt(
        jnp.maximum((2.0 * degree - 1.0) * (2.0 * degree + 1.0), 0.0)
        / jnp.maximum(j * (j + 2.0 * order_value), 1.0)
    )
    beta = jnp.sqrt(
        jnp.maximum((j - 1.0) * (j - 1.0 + 2.0 * order_value), 0.0)
        / jnp.maximum((2.0 * degree - 3.0) * (2.0 * degree - 1.0), 1.0)
    )
    moving = degree_index > 0
    first[...] = jnp.where(moving, alpha, 0.0)
    second[...] = jnp.where(moving, -alpha * beta, 1.0)
    shape = (ROWS, SIDE)
    row, half = iota(shape, 0), iota(shape, 1) & 1
    held = slot_cycle(half, row)
    z = jnp.where(held >= 0, 4.0 * (64.0 - 2.0 * held.astype(F32)) / (3.0 * NPIX), 0.0)
    below_one = 1.0 - (1.0 - z * z)
    log_term = -below_one * (1.0 + below_one * (0.5 + below_one * (1.0 / 3.0)))
    full = jnp.full(shape, order_value, F32)
    seed = jnp.exp(
        0.5 * jnp.log((2.0 * full + 1.0) / (4.0 * math.pi))
        - 0.25 * jnp.log(math.pi * (full + 0.25))
        + 0.5 * full * log_term
    )

    unroll = 8

    def compose(block, state):
        pu, pl_, qu, ql = state
        for s in range(unroll):
            i = block * unroll + s
            zc = z * first[pl.ds(i, 1), :]
            c2 = second[pl.ds(i, 1), :]
            pu, pl_ = zc * pu + c2 * pl_, pu
            qu, ql = zc * qu + c2 * ql, qu
        return pu, pl_, qu, ql

    fetch_row.wait()
    make_basis(orders_row, turns, basis, basis_turned, small_out)
    ones, zeros = jnp.ones(shape, F32), jnp.zeros(shape, F32)
    a, c, b, d = lax.fori_loop(0, SIDE // unroll, compose, (ones, zeros, zeros, ones))
    lanes = iota(shape, 1)
    for by in (2, 4, 8, 16, 32, 64):
        inside = lanes >= by
        ea = jnp.where(inside, pltpu.roll(a, by, 1), 1.0)
        eb = jnp.where(inside, pltpu.roll(b, by, 1), 0.0)
        ec = jnp.where(inside, pltpu.roll(c, by, 1), 0.0)
        ed = jnp.where(inside, pltpu.roll(d, by, 1), 1.0)
        a, b, c, d = a * ea + b * ec, a * eb + b * ed, c * ea + d * ec, c * eb + d * ed
    started = lanes >= 2
    upper = jnp.where(started, pltpu.roll(b, 2, 1) * seed, 0.0)
    lower = jnp.where(started, pltpu.roll(d, 2, 1) * seed, seed)

    fetch_harmonics.wait()
    valid = degree_index < LMAX - order
    even_lane = (lane & 1) == 0
    for r in range(2):
        turned = harmonics[r].T
        real = jnp.where(even_lane, turned, pltpu.roll(turned, 1, 1))
        imag = jnp.where(even_lane, pltpu.roll(turned, SIDE - 1, 1), turned)
        coefficients[2 * r] = jnp.where(valid, real, 0.0)
        coefficients[2 * r + 1] = jnp.where(valid, imag, 0.0)

    def advance(block, state):
        upper, lower, sums = state[0], state[1], list(state[2:])
        for s in range(unroll):
            i = block * unroll + s
            zc = z * first[pl.ds(i, 1), :]
            upper, lower = zc * upper + second[pl.ds(i, 1), :] * lower, upper
            table[i] = upper
            for f in range(4):
                at = 4 * (s % 2) + f
                sums[at] = sums[at] + coefficients[f, pl.ds(i, 1), :] * upper
        return (upper, lower, *sums)

    state = lax.fori_loop(0, SIDE // unroll, advance, (upper, lower) + (zeros,) * 8)
    sums = state[2:]
    high, low = split(jnp.concatenate(sums, axis=0))
    alike = ((iota(square, 0) & 1) == (iota(square, 1) & 1)).astype(BF16)
    sums = mxu(jnp.concatenate([high, low], axis=1), jnp.concatenate([alike, alike], axis=0))
    small = (2 * ROWS, SIDE)
    pair, lane_half = iota(small, 1) >> 1, iota(small, 1) & 1
    held_sums = jnp.zeros(small, F32)
    for f in range(4):
        both = [sums[(4 * parity + f) * ROWS : (4 * parity + f + 1) * ROWS] for parity in range(2)]
        held_sums = jnp.where(pair == f, jnp.concatenate(both, axis=0), held_sums)
    halves = jnp.concatenate([jnp.where(lane_half == half, held_sums, 0.0) for half in range(2)], axis=0)
    high, low = split(halves)
    sel = (2 * CYCLES, 4 * ROWS)
    at_row = iota(sel, 1)
    in_half = (at_row >= 2 * ROWS).astype(jnp.int32)
    at_row = at_row - 2 * ROWS * in_half
    odd = (at_row >= ROWS).astype(jnp.int32)
    pick = selection(iota(sel, 0) >> 1, odd == 1, in_half, at_row - ROWS * odd).astype(BF16)
    own = mxu(jnp.concatenate([pick, pick], axis=1), jnp.concatenate([high, low], axis=0))
    even_lane = (iota(square, 1) & 1) == 0
    own = own + jnp.where(even_lane, pltpu.roll(own, SIDE - 1, 1), pltpu.roll(own, 1, 1))
    own = jnp.where(iota(square, 1) < 8, own, 0.0)
    before = pltpu.roll(own, 2, 0)
    after = pltpu.roll(own, 2 * CYCLES - 2, 0)
    sent[...] = own + pltpu.roll(before, 8, 1) + pltpu.roll(after, 16, 1)


def both_halves(a, pair):
    product = mxu(jnp.concatenate(split(a), axis=1), jnp.concatenate([pair, pair], axis=0))
    return product[:, :SIDE] + product[:, SIDE:]


def swapped(x):
    x = jnp.broadcast_to(x, (8, SIDE))
    even = (iota((8, SIDE), 1) & 1) == 0
    return jnp.where(even, pltpu.roll(x, SIDE - 1, 1), pltpu.roll(x, 1, 1))[:1]


def neighbour(x, by):
    lane = iota((SIDE, SIDE), 1)
    if by == 1:
        moved = pltpu.roll(x, SIDE - 1, 1)
        return jnp.where(lane == SIDE - 1, pltpu.roll(moved, SIDE - 1, 0), moved)
    moved = pltpu.roll(x, 1, 1)
    return jnp.where(lane == 0, pltpu.roll(moved, 1, 0), moved)


def euler_kernel(weights_in, turns, basis, basis_turned, small, received, noise_in, within, across, kappa_out, sent,
                 fields, counts, level_weights, noise, kappa, sems):
    fetch_weights = pltpu.make_async_copy(weights_in, level_weights, sems.at[0])
    fetch_noise = pltpu.make_async_copy(noise_in, noise, sems.at[1])
    fetch_weights.start()
    fetch_noise.start()
    cycle = lax.axis_index("ma")
    parity = (cycle + 1 + NPIX // 4 - CYCLES // 2) % 2
    square = (SIDE, SIDE)
    row = iota(square, 0)
    a_cos, a_sin = turns[0], turns[1]
    spin_cos, spin_sin, weight = small[0, :1], small[1, :1], small[2, :1]
    low = (iota((1, SIDE), 1) & 1) == 0

    flipped = received[...].T
    lefts = []
    for kk in range(3):
        turned = parity == 1 if kk == 0 else parity == 0
        cs = jnp.where(turned, spin_cos, 1.0)
        sn = jnp.where(turned, spin_sin, 0.0)
        for r in range(2):
            real = flipped[8 * kk + 4 * r : 8 * kk + 4 * r + 1]
            imag = flipped[8 * kk + 4 * r + 2 : 8 * kk + 4 * r + 3]
            c_real = weight * (real * cs - imag * sn)
            c_imag = weight * (real * sn + imag * cs)
            u = jnp.where(low, c_real, -c_imag)
            v = jnp.where(low, -c_imag, -c_real)
            lefts.append(u * a_cos + v * a_sin)
    maps = both_halves(jnp.concatenate(lefts, axis=0), basis[...])

    for r in range(2):
        kappa[r] = maps[r * SIDE : (r + 1) * SIDE]
    keep_kappa = pltpu.make_async_copy(kappa, kappa_out, sems.at[2])
    keep_kappa.start()
    fetch_noise.wait()

    second_of_chip = cycle % 2 == 1
    noise_before = jnp.where(second_of_chip, within[...], across[...])
    noise_after = jnp.where(second_of_chip, across[...], within[...])

    def ratio(kk, r, weights):
        return 2.0 * (maps[(2 * kk + r) * SIDE : (2 * kk + r + 1) * SIDE] * weights)

    odd = parity == 1

    def aside(x):
        by = jnp.where(odd, SIDE - 1, 1)
        moved = pltpu.roll(x, by, 1)
        edge = jnp.where(odd, SIDE - 1, 0)
        return jnp.where(iota(square, 1) == edge, pltpu.roll(moved, by, 0), moved)

    for r in range(2):
        here = ratio(0, r, noise[...])
        above = jnp.where(cycle > 0, ratio(1, r, noise_before), FAR)
        below = jnp.where(cycle < CYCLES - 1, ratio(2, r, noise_after), FAR)
        fields[r, 0] = here
        fields[r, 1] = neighbour(here, 1)
        fields[r, 2] = neighbour(here, -1)
        moved_below, moved_above = aside(below), aside(above)
        fields[r, 3] = jnp.where(odd, below, moved_below)
        fields[r, 4] = jnp.where(odd, moved_below, below)
        fields[r, 5] = jnp.where(odd, above, moved_above)
        fields[r, 6] = jnp.where(odd, moved_above, above)

    counts[...] = jnp.zeros_like(counts)
    fetch_weights.wait()
    def sweep(top):
        for r in range(2):

            def tile(index, carry, r=r):
                at = pl.ds(pl.multiple_of(index * TILE, TILE), TILE)
                held = [fields[r, n, at, :] for n in range(5 if top else 7)]
                total = jnp.zeros((TILE, SIDE), F32)
                for t in range(LEVELS):
                    twice = 2.0 * (-3.0 + 6.0 * t / (LEVELS - 1))
                    u, e, w, d, dd, *others = [jnp.tanh(x - twice) for x in held]
                    n1, n2 = others if others else (-1.0, -1.0)
                    down = dd * (d + e)
                    up = 1.0 - e if top else n2 * (e + n1)
                    inner = down + up + w * (d + n1) - 2.0
                    scaled = level_weights[r, t] * u
                    total = total + inner * (level_weights[r, t] - scaled * u)
                    part = u * (2.0 - down - up) if top else u * (2.0 - down)
                    counts[r * LEVELS + t] += jnp.sum(part.reshape(TILE // 8, 8, SIDE), axis=0)
                fields[r, 0, at, :] = total
                return carry

            lax.fori_loop(0, SIDE // TILE, tile, 0)

    pl.when(cycle == 0)(lambda: sweep(True))
    pl.when(cycle > 0)(lambda: sweep(False))

    scale = 1.0 / (4.0 * math.sqrt(CYCLES * NPIX))
    duals = []
    gradients = jnp.concatenate([fields[r, 0] * (noise[...] * scale) for r in range(2)], axis=0)
    all_sums = both_halves(gradients, basis_turned[...])
    for r in range(2):
        sums = all_sums[r * SIDE : (r + 1) * SIDE]
        near = jnp.sum(sums * a_cos, axis=0, keepdims=True)
        far = jnp.sum(sums * a_sin, axis=0, keepdims=True)
        far = swapped(far)
        both = near + jnp.where(low, -far, far)
        other = swapped(both)
        cs = jnp.where(parity == 1, spin_cos, 1.0)
        sn = jnp.where(parity == 1, spin_sin, 0.0)
        duals.append(
            weight * jnp.where(low, both * cs - other * sn, -(both * cs + other * sn))
        )
    stacked = jnp.where(row == 0, duals[0], jnp.where(row == 1, duals[1], 0.0)).T
    level_sums = jnp.sum(counts[...], axis=1) * -0.125
    level_sums = level_sums + jnp.where(cycle == 0, 2.0 * NPIX / 8.0 / SIDE, 0.0)
    padded = jnp.concatenate([jnp.zeros_like(level_sums), level_sums], axis=0)
    level_row = dot(jnp.ones((8, SIDE), F32), padded, (1, 1))[:1]
    sent[...] = stacked + level_row
    keep_kappa.wait()


def adjoint_kernel(order_rows, received, table, gradient, turned):
    order = order_rows[:1]
    square = (SIDE, SIDE)
    lane, row = iota(square, 1), iota(square, 0)
    arrived = jnp.where(lane < CYCLES, received[...], 0.0)
    real = (row & 1) == 0
    pairs = jnp.where(real, arrived, 0.0) + pltpu.roll(jnp.where(real, 0.0, arrived), 2, 1)
    sel = (4 * ROWS, SIDE)
    at_row = iota(sel, 0)
    odd = (at_row >= 2 * ROWS).astype(jnp.int32)
    at_row = at_row - 2 * ROWS * odd
    in_half = (at_row >= ROWS).astype(jnp.int32)
    pick = selection(iota(sel, 1) >> 1, odd == 1, in_half, at_row - ROWS * in_half).astype(BF16)
    duals = mxu(jnp.concatenate([pick, pick], axis=1), jnp.concatenate(split(pairs), axis=0))
    even = (iota((ROWS, SIDE), 1) & 1) == 0

    def column(parity, half, r, c):
        start = (2 * parity + half) * ROWS
        at = 2 * c + r
        return jnp.broadcast_to(duals[start : start + ROWS, at : at + 1], (ROWS, SIDE))

    factors = [
        [
            (
                jnp.where(even, column(parity, 0, r, 0), column(parity, 1, r, 1)),
                jnp.where(even, column(parity, 0, r, 1), column(parity, 1, r, 0)),
            )
            for r in range(2)
        ]
        for parity in range(2)
    ]

    sub = iota((8, SIDE), 0)

    def merge(a, b, by):
        mine = (sub & by) == 0
        return jnp.where(mine, a, b) + pltpu.roll(jnp.where(mine, b, a), 8 - by, 0)

    even_lane = (iota((8, SIDE), 1) & 1) == 0

    def block(index, carry):
        at = pl.ds(pl.multiple_of(index * 8, 8), 8)
        values = [table[index * 8 + s] for s in range(8)]
        for r in range(2):
            summed = []
            for kind in range(2):
                parts = []
                for s in range(8):
                    product = values[s] * factors[s % 2][r][kind]
                    parts.append(product[:8] + product[8:16] + product[16:])
                for by in (1, 2, 4):
                    parts = [merge(a, b, by) for a, b in zip(parts[::2], parts[1::2])]
                summed.append(parts[0])
            straight, crossed = summed
            crossed = jnp.where(even_lane, pltpu.roll(crossed, SIDE - 1, 1), pltpu.roll(crossed, 1, 1))
            turned[r, at, :] = straight + crossed
        return carry

    lax.fori_loop(0, SIDE // 8, block, 0)
    for r in range(2):
        degree_index = (row >> 1) * SIDE + lane
        gradient[r] = jnp.where(degree_index < LMAX - order, turned[r].T, 0.0)


VMEM = pl.BlockSpec(memory_space=pltpu.VMEM)
SMEM = pl.BlockSpec(memory_space=pltpu.SMEM)
HBM = pl.BlockSpec(memory_space=pltpu.HBM)
PARAMS = pltpu.CompilerParams(vmem_limit_bytes=40 * 1024 * 1024)


def shards(harmonics, noise_weight, order_table, curve_weight):
    ta_count = lax.axis_size("ta")
    ma_count = lax.axis_size("ma")
    noise = noise_weight.reshape(SIDE, SIDE)
    within = lax.ppermute(noise, "ma", [(i, i ^ 1) for i in range(ma_count)])
    across = lax.ppermute(noise, "ma", [(i, i + 1 if i % 2 else i - 1) for i in range(1, ma_count - 1)])
    packed = harmonics.reshape(2, 2, 64, SIDE).transpose(0, 2, 1, 3).reshape(2, SIDE, SIDE)
    square = jax.ShapeDtypeStruct((2 * CYCLES, SIDE), F32)
    orders_there = pltpu.with_memory_space_constraint(order_table, pltpu.HBM)
    packed = pltpu.with_memory_space_constraint(packed, pltpu.HBM)
    table, sent, order_rows, turns, basis, basis_turned, small = pl.pallas_call(
        legendre_kernel,
        in_specs=[HBM, HBM, HBM],
        out_specs=[VMEM] * 7,
        out_shape=[
            jax.ShapeDtypeStruct((SIDE, ROWS, SIDE), F32),
            square,
            jax.ShapeDtypeStruct((8, SIDE), jnp.int32),
            jax.ShapeDtypeStruct((2, SIDE, SIDE), F32),
            jax.ShapeDtypeStruct((SIDE, 2 * SIDE), BF16),
            jax.ShapeDtypeStruct((SIDE, 2 * SIDE), BF16),
            jax.ShapeDtypeStruct((3, 8, SIDE), F32),
        ],
        scratch_shapes=[
            pltpu.VMEM((SIDE, SIDE), F32),
            pltpu.VMEM((SIDE, SIDE), F32),
            pltpu.VMEM((4, SIDE, SIDE), F32),
            pltpu.SMEM((CYCLES,), jnp.int32),
            pltpu.VMEM((2, SIDE, SIDE), F32),
            pltpu.VMEM((1, CYCLES), jnp.int32),
            pltpu.SemaphoreType.DMA((3,)),
        ],
        compiler_params=PARAMS,
        name="legendre",
    )(orders_there, pltpu.with_memory_space_constraint(order_table.reshape(1, CYCLES), pltpu.HBM), packed)
    sent, within, across = lax.optimization_barrier((sent, within, across))
    received = lax.all_to_all(sent, "ma", split_axis=0, concat_axis=0, tiled=True)
    kappa, sent = pl.pallas_call(
        euler_kernel,
        in_specs=[HBM, VMEM, VMEM, VMEM, VMEM, VMEM, HBM, VMEM, VMEM],
        out_specs=[HBM, VMEM],
        out_shape=[jax.ShapeDtypeStruct((2, SIDE, SIDE), F32), square],
        scratch_shapes=[
            pltpu.VMEM((2, 7, SIDE, SIDE), F32),
            pltpu.VMEM((2 * LEVELS, 8, SIDE), F32),
            pltpu.SMEM((2, LEVELS), F32),
            pltpu.VMEM((SIDE, SIDE), F32),
            pltpu.VMEM((2, SIDE, SIDE), F32),
            pltpu.SemaphoreType.DMA((3,)),
        ],
        compiler_params=PARAMS,
        name="euler",
    )(
        pltpu.with_memory_space_constraint(curve_weight, pltpu.HBM),
        turns,
        basis,
        basis_turned,
        small,
        received,
        pltpu.with_memory_space_constraint(noise, pltpu.HBM),
        within, across)
    received = lax.all_to_all(sent, "ma", split_axis=0, concat_axis=0, tiled=True)
    counts = jnp.sum(received.reshape(CYCLES, 2, SIDE)[:, 0, CYCLES:], axis=0).reshape(2, LEVELS)
    one, two, three = [lax.ppermute(counts, "ta", [(i, i ^ by) for i in range(ta_count)]) for by in (1, 2, 3)]
    curve = ((counts + one) + (two + three)) / (ta_count * CYCLES * NPIX)
    gradient = pl.pallas_call(
        adjoint_kernel,
        in_specs=[VMEM, VMEM, VMEM],
        out_specs=VMEM,
        out_shape=jax.ShapeDtypeStruct((2, SIDE, SIDE), F32),
        scratch_shapes=[pltpu.VMEM((2, SIDE, SIDE), F32)],
        compiler_params=PARAMS,
        name="adjoint",
    )(order_rows, received, table)
    gradient = gradient.reshape(2, 64, 2, SIDE).transpose(0, 2, 1, 3).reshape(1, 2, 1, 2, LMAX)
    return kappa.reshape(1, 2, 1, NPIX), curve, gradient


def solution(mesh):
    in_specs = (P("ta", None, "ma", None, None), P("ta", "ma", None), P(), P())
    out_specs = (P("ta", None, "ma", None), P(), P("ta", None, "ma", None, None))
    return jax.shard_map(shards, mesh=mesh, in_specs=in_specs, out_specs=out_specs, check_vma=False)
```

```python
import math

import jax
import jax.numpy as jnp
from jax import lax
from jax.experimental import pallas as pl
from jax.experimental.pallas import tpu as pltpu
from jax.sharding import PartitionSpec as P

F32 = jnp.float32
BF16 = jnp.bfloat16
HIGHEST = lax.Precision.HIGHEST
NPIX = 16384
LMAX = 8192
CYCLES = 64
LEVELS = 32
SIDE = 128
ROWS = 24
TILE = 16
FAR = -1.0e9


def iota(shape, dim):
    return lax.broadcasted_iota(jnp.int32, shape, dim)


def dot(a, b, contract):
    return lax.dot_general(a, b, ((contract[:1], contract[1:]), ((), ())), precision=HIGHEST,
                           preferred_element_type=F32)


def slot_cycle(half, row):
    own = jnp.where(row < 16, row + 16 * half, -1)
    return jnp.where((row == 16) & (half == 0), 32, own)


def selection(cycle, odd, half, row):
    mirrored = jnp.where(cycle > 32, 64 - cycle, cycle)
    sign = jnp.where((cycle > 32) & odd, -1.0, 1.0)
    return jnp.where(slot_cycle(half, row) == mirrored, sign, 0.0).astype(F32)


def split(x):
    high = x.astype(BF16)
    return high, (x - high.astype(F32)).astype(BF16)


def mxu(a, b):
    return lax.dot_general(a, b, (((1,), (0,)), ((), ())), preferred_element_type=F32)


def turn_cos_sin(index, whole):
    quarter = whole // 4
    index = index & (whole - 1)
    quadrant = (index + quarter // 2) >> (quarter.bit_length() - 1)
    x = (index - quadrant * quarter).astype(F32) * (2.0 * math.pi / whole)
    y = x * x
    sine = x * (1.0 + y * (-1.0 / 6 + y * (1.0 / 120 + y * (-1.0 / 5040 + y * (1.0 / 362880)))))
    cosine = 1.0 + y * (-0.5 + y * (1.0 / 24 + y * (-1.0 / 720 + y * (1.0 / 40320 - y * (1.0 / 3628800)))))
    swap = (quadrant & 1) == 1
    c = jnp.where(swap, sine, cosine)
    s = jnp.where(swap, cosine, sine)
    c = jnp.where(((quadrant + 1) & 2) == 2, -c, c)
    s = jnp.where((quadrant & 2) == 2, -s, s)
    return c, s


def make_basis(orders_row, turns, basis, basis_turned, small):
    square = (SIDE, SIDE)
    lane, row = iota(square, 1), iota(square, 0)
    twice = (iota((CYCLES, SIDE), 1) >> 1) == iota((CYCLES, SIDE), 0)
    eight = jnp.broadcast_to(orders_row[...].astype(F32), (8, CYCLES))
    eight = dot(eight, twice.astype(F32), (1, 0)).astype(jnp.int32)
    orders = jnp.broadcast_to(eight[:1], square)
    turns[0], turns[1] = turn_cos_sin(orders * row, SIDE)
    cosine, sine = turn_cos_sin(orders * row, NPIX)
    turned = jnp.where((lane & 1) == 0, cosine, sine)
    for ref, value in ((basis, turned.T), (basis_turned, turned)):
        ref[:, :SIDE], ref[:, SIDE:] = split(value)
    small[0], small[1] = turn_cos_sin(eight, 2 * NPIX)
    small[2] = jnp.where(eight == 0, 1.0, 2.0)


def legendre_kernel(orders_in, row_in, harmonics_in, noise_in, weights_in, table, sent, order_out, turns, basis, basis_turned,
                    small_out, noise, weights,
                    first, second, coefficients, orders, harmonics, orders_row, picked, sems):
    ma = lax.axis_index("ma")
    fetch_orders = pltpu.make_async_copy(orders_in, orders, sems.at[0])
    fetch_harmonics = pltpu.make_async_copy(harmonics_in, harmonics, sems.at[1])
    fetch_row = pltpu.make_async_copy(row_in, orders_row, sems.at[2])
    fetch_orders.start()
    fetch_row.start()
    fetch_harmonics.start()
    fetch_noise = pltpu.make_async_copy(noise_in, noise, sems.at[3])
    fetch_weights = pltpu.make_async_copy(weights_in, weights, sems.at[4])
    fetch_noise.start()
    fetch_weights.start()
    square = (SIDE, SIDE)
    alike = ((iota(square, 0) & 1) == (iota(square, 1) & 1)).astype(BF16)
    sel = (2 * CYCLES, 4 * ROWS)
    column = iota(sel, 1)
    in_half = (column >= 2 * ROWS).astype(jnp.int32)
    column = column - 2 * ROWS * in_half
    odd = (column >= ROWS).astype(jnp.int32)
    picked[...] = selection(iota(sel, 0) >> 1, odd == 1, in_half, column - ROWS * odd).astype(BF16)
    shape = (ROWS, SIDE)
    row, half = iota(shape, 0), iota(shape, 1) & 1
    held = slot_cycle(half, row)
    z = jnp.where(held >= 0, 4.0 * (64.0 - 2.0 * held.astype(F32)) / (3.0 * NPIX), 0.0)
    below_one = 1.0 - (1.0 - z * z)
    log_term = -below_one * (1.0 + below_one * (0.5 + below_one * (1.0 / 3.0)))
    fetch_orders.wait()
    order = orders[ma]
    order_out[...] = jnp.full(order_out.shape, order, jnp.int32)
    order_value = order.astype(F32)
    square = (SIDE, SIDE)
    lane, step = iota(square, 1), iota(square, 0)
    degree_index = (lane >> 1) * SIDE + step
    j = degree_index.astype(F32)
    degree = order_value + j
    alpha = jnp.sqrt(
        jnp.maximum((2.0 * degree - 1.0) * (2.0 * degree + 1.0), 0.0)
        / jnp.maximum(j * (j + 2.0 * order_value), 1.0)
    )
    beta = jnp.sqrt(
        jnp.maximum((j - 1.0) * (j - 1.0 + 2.0 * order_value), 0.0)
        / jnp.maximum((2.0 * degree - 3.0) * (2.0 * degree - 1.0), 1.0)
    )
    moving = degree_index > 0
    first[...] = jnp.where(moving, alpha, 0.0)
    second[...] = jnp.where(moving, -alpha * beta, 1.0)
    full = jnp.full(shape, order_value, F32)
    seed = jnp.exp(
        0.5 * jnp.log((2.0 * full + 1.0) / (4.0 * math.pi))
        - 0.25 * jnp.log(math.pi * (full + 0.25))
        + 0.5 * full * log_term
    )

    unroll = 16

    def compose(block, state):
        pu, pl_, qu, ql = state
        for s in range(unroll):
            i = block * unroll + s
            zc = z * first[pl.ds(i, 1), :]
            c2 = second[pl.ds(i, 1), :]
            pu, pl_ = zc * pu + c2 * pl_, pu
            qu, ql = zc * qu + c2 * ql, qu
        return pu, pl_, qu, ql

    fetch_row.wait()
    make_basis(orders_row, turns, basis, basis_turned, small_out)
    ones, zeros = jnp.ones(shape, F32), jnp.zeros(shape, F32)
    a, c, b, d = lax.fori_loop(0, SIDE // unroll, compose, (ones, zeros, zeros, ones))
    lanes = iota(shape, 1)
    for by in (2, 4, 8, 16, 32, 64):
        inside = lanes >= by
        ea = jnp.where(inside, pltpu.roll(a, by, 1), 1.0)
        eb = jnp.where(inside, pltpu.roll(b, by, 1), 0.0)
        ec = jnp.where(inside, pltpu.roll(c, by, 1), 0.0)
        ed = jnp.where(inside, pltpu.roll(d, by, 1), 1.0)
        a, b, c, d = a * ea + b * ec, a * eb + b * ed, c * ea + d * ec, c * eb + d * ed
    started = lanes >= 2
    upper = jnp.where(started, pltpu.roll(b, 2, 1) * seed, 0.0)
    lower = jnp.where(started, pltpu.roll(d, 2, 1) * seed, seed)

    fetch_harmonics.wait()
    valid = degree_index < LMAX - order
    even_lane = (lane & 1) == 0
    for r in range(2):
        turned = harmonics[r].T
        real = jnp.where(even_lane, turned, pltpu.roll(turned, 1, 1))
        imag = jnp.where(even_lane, pltpu.roll(turned, SIDE - 1, 1), turned)
        coefficients[2 * r] = jnp.where(valid, real, 0.0)
        coefficients[2 * r + 1] = jnp.where(valid, imag, 0.0)

    def advance(block, state):
        upper, lower, sums = state[0], state[1], list(state[2:])
        for s in range(unroll):
            i = block * unroll + s
            zc = z * first[pl.ds(i, 1), :]
            upper, lower = zc * upper + second[pl.ds(i, 1), :] * lower, upper
            table[i] = upper
            for f in range(4):
                at = 4 * (s % 2) + f
                sums[at] = sums[at] + coefficients[f, pl.ds(i, 1), :] * upper
        return (upper, lower, *sums)

    state = lax.fori_loop(0, SIDE // unroll, advance, (upper, lower) + (zeros,) * 8)
    sums = state[2:]
    high, low = split(jnp.concatenate(sums, axis=0))
    sums = mxu(jnp.concatenate([high, low], axis=1), jnp.concatenate([alike, alike], axis=0))
    small = (2 * ROWS, SIDE)
    pair, lane_half = iota(small, 1) >> 1, iota(small, 1) & 1
    held_sums = jnp.zeros(small, F32)
    for f in range(4):
        both = [sums[(4 * parity + f) * ROWS : (4 * parity + f + 1) * ROWS] for parity in range(2)]
        held_sums = jnp.where(pair == f, jnp.concatenate(both, axis=0), held_sums)
    halves = jnp.concatenate([jnp.where(lane_half == half, held_sums, 0.0) for half in range(2)], axis=0)
    high, low = split(halves)
    own = mxu(jnp.concatenate([picked[...], picked[...]], axis=1), jnp.concatenate([high, low], axis=0))
    even_lane = (iota(square, 1) & 1) == 0
    own = own + jnp.where(even_lane, pltpu.roll(own, SIDE - 1, 1), pltpu.roll(own, 1, 1))
    own = jnp.where(iota(square, 1) < 8, own, 0.0)
    before = pltpu.roll(own, 2, 0)
    after = pltpu.roll(own, 2 * CYCLES - 2, 0)
    sent[...] = own + pltpu.roll(before, 8, 1) + pltpu.roll(after, 16, 1)
    fetch_noise.wait()
    fetch_weights.wait()


def both_halves(a, pair):
    product = mxu(jnp.concatenate(split(a), axis=1), jnp.concatenate([pair, pair], axis=0))
    return product[:, :SIDE] + product[:, SIDE:]


def swapped(x):
    x = jnp.broadcast_to(x, (8, SIDE))
    even = (iota((8, SIDE), 1) & 1) == 0
    return jnp.where(even, pltpu.roll(x, SIDE - 1, 1), pltpu.roll(x, 1, 1))[:1]


def neighbour(x, by):
    lane = iota((SIDE, SIDE), 1)
    if by == 1:
        moved = pltpu.roll(x, SIDE - 1, 1)
        return jnp.where(lane == SIDE - 1, pltpu.roll(moved, SIDE - 1, 0), moved)
    moved = pltpu.roll(x, 1, 1)
    return jnp.where(lane == 0, pltpu.roll(moved, 1, 0), moved)


def euler_kernel(level_weights, turns, basis, basis_turned, small, received, noise, within, across, kappa_out, sent,
                 fields, counts, kappa, sems):
    cycle = lax.axis_index("ma")
    parity = (cycle + 1 + NPIX // 4 - CYCLES // 2) % 2
    square = (SIDE, SIDE)
    row = iota(square, 0)
    a_cos, a_sin = turns[0], turns[1]
    spin_cos, spin_sin, weight = small[0, :1], small[1, :1], small[2, :1]
    low = (iota((1, SIDE), 1) & 1) == 0

    flipped = received[...].T
    lefts = []
    for kk in range(3):
        turned = parity == 1 if kk == 0 else parity == 0
        cs = jnp.where(turned, spin_cos, 1.0)
        sn = jnp.where(turned, spin_sin, 0.0)
        for r in range(2):
            real = flipped[8 * kk + 4 * r : 8 * kk + 4 * r + 1]
            imag = flipped[8 * kk + 4 * r + 2 : 8 * kk + 4 * r + 3]
            c_real = weight * (real * cs - imag * sn)
            c_imag = weight * (real * sn + imag * cs)
            u = jnp.where(low, c_real, -c_imag)
            v = jnp.where(low, -c_imag, -c_real)
            lefts.append(u * a_cos + v * a_sin)
    maps = both_halves(jnp.concatenate(lefts, axis=0), basis[...])

    for r in range(2):
        kappa[r] = maps[r * SIDE : (r + 1) * SIDE]
    keep_kappa = pltpu.make_async_copy(kappa, kappa_out, sems.at[0])
    keep_kappa.start()

    second_of_chip = cycle % 2 == 1
    noise_before = jnp.where(second_of_chip, within[...], across[...])
    noise_after = jnp.where(second_of_chip, across[...], within[...])

    def ratio(kk, r, weights):
        return 2.0 * (maps[(2 * kk + r) * SIDE : (2 * kk + r + 1) * SIDE] * weights)

    odd = parity == 1

    def aside(x):
        by = jnp.where(odd, SIDE - 1, 1)
        moved = pltpu.roll(x, by, 1)
        edge = jnp.where(odd, SIDE - 1, 0)
        return jnp.where(iota(square, 1) == edge, pltpu.roll(moved, by, 0), moved)

    for r in range(2):
        here = ratio(0, r, noise[...])
        above = jnp.where(cycle > 0, ratio(1, r, noise_before), FAR)
        below = jnp.where(cycle < CYCLES - 1, ratio(2, r, noise_after), FAR)
        fields[r, 0] = here
        fields[r, 1] = neighbour(here, 1)
        fields[r, 2] = neighbour(here, -1)
        moved_below, moved_above = aside(below), aside(above)
        fields[r, 3] = jnp.where(odd, below, moved_below)
        fields[r, 4] = jnp.where(odd, moved_below, below)
        fields[r, 5] = jnp.where(odd, above, moved_above)
        fields[r, 6] = jnp.where(odd, moved_above, above)

    counts[...] = jnp.zeros_like(counts)
    def sweep(top):
        def tile(index, r):
            at = pl.ds(pl.multiple_of(index * TILE, TILE), TILE)
            held = [fields[r, n, at, :] for n in range(5 if top else 7)]
            total = jnp.zeros((TILE, SIDE), F32)
            for t in range(LEVELS):
                twice = 2.0 * (-3.0 + 6.0 * t / (LEVELS - 1))
                u, e, w, d, dd, *others = [jnp.tanh(x - twice) for x in held]
                n1, n2 = others if others else (-1.0, -1.0)
                down = dd * (d + e)
                up = 1.0 - e if top else n2 * (e + n1)
                inner = down + up + w * (d + n1) - 2.0
                scaled = level_weights[r, t] * u
                total = total + inner * (level_weights[r, t] - scaled * u)
                part = u * (2.0 - down - up) if top else u * (2.0 - down)
                counts[r * LEVELS + t] += jnp.sum(part.reshape(TILE // 8, 8, SIDE), axis=0)
            fields[r, 0, at, :] = total

        def tiles(index, carry):
            for more in range(1):
                for r in range(2):
                    tile(index * 1 + more, r)
            return carry

        lax.fori_loop(0, SIDE // TILE // 1, tiles, 0)

    pl.when(cycle == 0)(lambda: sweep(True))
    pl.when(cycle > 0)(lambda: sweep(False))

    scale = 1.0 / (4.0 * math.sqrt(CYCLES * NPIX))
    duals = []
    gradients = jnp.concatenate([fields[r, 0] * (noise[...] * scale) for r in range(2)], axis=0)
    all_sums = both_halves(gradients, basis_turned[...])
    for r in range(2):
        sums = all_sums[r * SIDE : (r + 1) * SIDE]
        near = jnp.sum(sums * a_cos, axis=0, keepdims=True)
        far = jnp.sum(sums * a_sin, axis=0, keepdims=True)
        far = swapped(far)
        both = near + jnp.where(low, -far, far)
        other = swapped(both)
        cs = jnp.where(parity == 1, spin_cos, 1.0)
        sn = jnp.where(parity == 1, spin_sin, 0.0)
        duals.append(
            weight * jnp.where(low, both * cs - other * sn, -(both * cs + other * sn))
        )
    stacked = jnp.where(row == 0, duals[0], jnp.where(row == 1, duals[1], 0.0)).T
    level_sums = jnp.sum(counts[...], axis=1) * -0.125
    level_sums = level_sums + jnp.where(cycle == 0, 2.0 * NPIX / 8.0 / SIDE, 0.0)
    padded = jnp.concatenate([jnp.zeros_like(level_sums), level_sums], axis=0)
    level_row = dot(jnp.ones((8, SIDE), F32), padded, (1, 1))[:1]
    sent[...] = stacked + level_row
    keep_kappa.wait()


def adjoint_kernel(order_rows, received, table, gradient, turned):
    order = order_rows[:1]
    square = (SIDE, SIDE)
    lane, row = iota(square, 1), iota(square, 0)
    arrived = jnp.where(lane < CYCLES, received[...], 0.0)
    real = (row & 1) == 0
    pairs = jnp.where(real, arrived, 0.0) + pltpu.roll(jnp.where(real, 0.0, arrived), 2, 1)
    sel = (4 * ROWS, SIDE)
    at_row = iota(sel, 0)
    odd = (at_row >= 2 * ROWS).astype(jnp.int32)
    at_row = at_row - 2 * ROWS * odd
    in_half = (at_row >= ROWS).astype(jnp.int32)
    pick = selection(iota(sel, 1) >> 1, odd == 1, in_half, at_row - ROWS * in_half).astype(BF16)
    duals = mxu(jnp.concatenate([pick, pick], axis=1), jnp.concatenate(split(pairs), axis=0))
    even = (iota((ROWS, SIDE), 1) & 1) == 0

    def column(parity, half, r, c):
        start = (2 * parity + half) * ROWS
        at = 2 * c + r
        return jnp.broadcast_to(duals[start : start + ROWS, at : at + 1], (ROWS, SIDE))

    factors = [
        [
            (
                jnp.where(even, column(parity, 0, r, 0), column(parity, 1, r, 1)),
                jnp.where(even, column(parity, 0, r, 1), column(parity, 1, r, 0)),
            )
            for r in range(2)
        ]
        for parity in range(2)
    ]

    sub = iota((8, SIDE), 0)

    def merge(a, b, by):
        mine = (sub & by) == 0
        return jnp.where(mine, a, b) + pltpu.roll(jnp.where(mine, b, a), 8 - by, 0)

    even_lane = (iota((8, SIDE), 1) & 1) == 0

    def block(index):
        at = pl.ds(pl.multiple_of(index * 8, 8), 8)
        held = {}
        for s in range(8):
            value = table[index * 8 + s]
            for r in range(2):
                for kind in range(2):
                    product = value * factors[s % 2][r][kind]
                    part = product[:8] + product[8:16] + product[16:]
                    by = 1
                    while s & by:
                        part = merge(held.pop((r, kind, by)), part, by)
                        by *= 2
                    held[r, kind, by] = part
        for r in range(2):
            straight, crossed = held[r, 0, 8], held[r, 1, 8]
            crossed = jnp.where(even_lane, pltpu.roll(crossed, SIDE - 1, 1), pltpu.roll(crossed, 1, 1))
            turned[r, at, :] = straight + crossed

    def blocks(index, carry):
        for more in range(4):
            block(index * 4 + more)
        return carry

    lax.fori_loop(0, SIDE // 8 // 4, blocks, 0)
    for r in range(2):
        degree_index = (row >> 1) * SIDE + lane
        gradient[r] = jnp.where(degree_index < LMAX - order, turned[r].T, 0.0)


VMEM = pl.BlockSpec(memory_space=pltpu.VMEM)
SMEM = pl.BlockSpec(memory_space=pltpu.SMEM)
HBM = pl.BlockSpec(memory_space=pltpu.HBM)
PARAMS = pltpu.CompilerParams(vmem_limit_bytes=40 * 1024 * 1024)


def shards(harmonics, noise_weight, order_table, curve_weight):
    ta_count = lax.axis_size("ta")
    ma_count = lax.axis_size("ma")
    noise = noise_weight.reshape(SIDE, SIDE)
    within = lax.ppermute(noise, "ma", [(i, i ^ 1) for i in range(ma_count)])
    across = lax.ppermute(noise, "ma", [(i, i + 1 if i % 2 else i - 1) for i in range(1, ma_count - 1)])
    packed = harmonics.reshape(2, 2, 64, SIDE).transpose(0, 2, 1, 3).reshape(2, SIDE, SIDE)
    square = jax.ShapeDtypeStruct((2 * CYCLES, SIDE), F32)
    orders_there = pltpu.with_memory_space_constraint(order_table, pltpu.HBM)
    packed = pltpu.with_memory_space_constraint(packed, pltpu.HBM)
    table, sent, order_rows, turns, basis, basis_turned, small, noise_here, weights = pl.pallas_call(
        legendre_kernel,
        in_specs=[HBM] * 5,
        out_specs=[VMEM] * 9,
        out_shape=[
            jax.ShapeDtypeStruct((SIDE, ROWS, SIDE), F32),
            square,
            jax.ShapeDtypeStruct((8, SIDE), jnp.int32),
            jax.ShapeDtypeStruct((2, SIDE, SIDE), F32),
            jax.ShapeDtypeStruct((SIDE, 2 * SIDE), BF16),
            jax.ShapeDtypeStruct((SIDE, 2 * SIDE), BF16),
            jax.ShapeDtypeStruct((3, 8, SIDE), F32),
            jax.ShapeDtypeStruct((SIDE, SIDE), F32),
            jax.ShapeDtypeStruct((2, LEVELS), F32),
        ],
        scratch_shapes=[
            pltpu.VMEM((SIDE, SIDE), F32),
            pltpu.VMEM((SIDE, SIDE), F32),
            pltpu.VMEM((4, SIDE, SIDE), F32),
            pltpu.SMEM((CYCLES,), jnp.int32),
            pltpu.VMEM((2, SIDE, SIDE), F32),
            pltpu.VMEM((1, CYCLES), jnp.int32),
            pltpu.VMEM((2 * CYCLES, 4 * ROWS), BF16),
            pltpu.SemaphoreType.DMA((5,)),
        ],
        compiler_params=PARAMS,
        name="legendre",
    )(
        orders_there,
        pltpu.with_memory_space_constraint(order_table.reshape(1, CYCLES), pltpu.HBM),
        packed,
        pltpu.with_memory_space_constraint(noise, pltpu.HBM),
        pltpu.with_memory_space_constraint(curve_weight, pltpu.HBM),
    )
    sent, within, across = lax.optimization_barrier((sent, within, across))
    received = lax.all_to_all(sent, "ma", split_axis=0, concat_axis=0, tiled=True)
    kappa, sent = pl.pallas_call(
        euler_kernel,
        in_specs=[SMEM] + [VMEM] * 8,
        out_specs=[HBM, VMEM],
        out_shape=[jax.ShapeDtypeStruct((2, SIDE, SIDE), F32), square],
        scratch_shapes=[
            pltpu.VMEM((2, 7, SIDE, SIDE), F32),
            pltpu.VMEM((2 * LEVELS, 8, SIDE), F32),
            pltpu.VMEM((2, SIDE, SIDE), F32),
            pltpu.SemaphoreType.DMA((1,)),
        ],
        compiler_params=PARAMS,
        name="euler",
    )(
        weights,
        turns,
        basis,
        basis_turned,
        small,
        received,
        noise_here,
        within,
        across,
    )
    received = lax.all_to_all(sent, "ma", split_axis=0, concat_axis=0, tiled=True)
    counts = jnp.sum(received.reshape(CYCLES, 2, SIDE)[:, 0, CYCLES:], axis=0).reshape(2, LEVELS)
    one, two, three = [lax.ppermute(counts, "ta", [(i, i ^ by) for i in range(ta_count)]) for by in (1, 2, 3)]
    curve = ((counts + one) + (two + three)) / (ta_count * CYCLES * NPIX)
    gradient = pl.pallas_call(
        adjoint_kernel,
        in_specs=[VMEM, VMEM, VMEM],
        out_specs=VMEM,
        out_shape=jax.ShapeDtypeStruct((2, SIDE, SIDE), F32),
        scratch_shapes=[pltpu.VMEM((2, SIDE, SIDE), F32)],
        compiler_params=PARAMS,
        name="adjoint",
    )(order_rows, received, table)
    gradient = gradient.reshape(2, 64, 2, SIDE).transpose(0, 2, 1, 3).reshape(1, 2, 1, 2, LMAX)
    return kappa.reshape(1, 2, 1, NPIX), curve, gradient


def solution(mesh):
    in_specs = (P("ta", None, "ma", None, None), P("ta", "ma", None), P(), P())
    out_specs = (P("ta", None, "ma", None), P(), P("ta", None, "ma", None, None))
    return jax.shard_map(shards, mesh=mesh, in_specs=in_specs, out_specs=out_specs, check_vma=False)
```

```python
import math

import jax
import jax.numpy as jnp
from jax import lax
from jax.experimental import pallas as pl
from jax.experimental.pallas import tpu as pltpu
from jax.sharding import PartitionSpec as P

F32 = jnp.float32
BF16 = jnp.bfloat16
HIGHEST = lax.Precision.HIGHEST
NPIX = 16384
LMAX = 8192
CYCLES = 64
LEVELS = 32
SIDE = 128
ROWS = 24
GROUP = 4
FAR = -1.0e9


def iota(shape, dim):
    return lax.broadcasted_iota(jnp.int32, shape, dim)


def dot(a, b, contract):
    return lax.dot_general(a, b, ((contract[:1], contract[1:]), ((), ())), precision=HIGHEST,
                           preferred_element_type=F32)


def slot_cycle(half, row):
    own = jnp.where(row < 16, row + 16 * half, -1)
    return jnp.where((row == 16) & (half == 0), 32, own)


def selection(cycle, odd, half, row):
    mirrored = jnp.where(cycle > 32, 64 - cycle, cycle)
    sign = jnp.where((cycle > 32) & odd, -1.0, 1.0)
    return jnp.where(slot_cycle(half, row) == mirrored, sign, 0.0).astype(F32)


def split(x):
    high = x.astype(BF16)
    return high, (x - high.astype(F32)).astype(BF16)


def mxu(a, b):
    return lax.dot_general(a, b, (((1,), (0,)), ((), ())), preferred_element_type=F32)


def turn_cos_sin(index, whole):
    quarter = whole // 4
    index = index & (whole - 1)
    quadrant = (index + quarter // 2) >> (quarter.bit_length() - 1)
    x = (index - quadrant * quarter).astype(F32) * (2.0 * math.pi / whole)
    y = x * x
    sine = x * (1.0 + y * (-1.0 / 6 + y * (1.0 / 120 + y * (-1.0 / 5040 + y * (1.0 / 362880)))))
    cosine = 1.0 + y * (-0.5 + y * (1.0 / 24 + y * (-1.0 / 720 + y * (1.0 / 40320 - y * (1.0 / 3628800)))))
    swap = (quadrant & 1) == 1
    c = jnp.where(swap, sine, cosine)
    s = jnp.where(swap, cosine, sine)
    c = jnp.where(((quadrant + 1) & 2) == 2, -c, c)
    s = jnp.where((quadrant & 2) == 2, -s, s)
    return c, s


def make_basis(orders_row, turns, basis, basis_turned, small):
    square = (SIDE, SIDE)
    lane, row = iota(square, 1), iota(square, 0)
    twice = (iota((CYCLES, SIDE), 1) >> 1) == iota((CYCLES, SIDE), 0)
    eight = jnp.broadcast_to(orders_row[...].astype(F32), (8, CYCLES))
    eight = dot(eight, twice.astype(F32), (1, 0)).astype(jnp.int32)
    orders = jnp.broadcast_to(eight[:1], square)
    down = orders.astype(F32).T.astype(jnp.int32)
    turns[0], turns[1] = turn_cos_sin(down * lane, SIDE)
    pixel = 16 * (row & 7) + (row >> 3)
    cosine, sine = turn_cos_sin(orders * pixel, NPIX)
    turned = jnp.where((lane & 1) == 0, cosine, sine)
    for ref, value in ((basis, turned.T), (basis_turned, turned)):
        ref[:, :SIDE], ref[:, SIDE:] = split(value)
    small[0], small[1] = turn_cos_sin(down, 2 * NPIX)
    small[2] = jnp.where(down == 0, 1.0, 2.0)


def legendre_kernel(orders_in, row_in, harmonics_in, noise_in, weights_in, table, sent, order_out, turns, basis, basis_turned,
                    small_out, noise, weights,
                    first, second, coefficients, orders, harmonics, orders_row, picked, sems):
    ma = lax.axis_index("ma")
    fetch_orders = pltpu.make_async_copy(orders_in, orders, sems.at[0])
    fetch_harmonics = pltpu.make_async_copy(harmonics_in, harmonics, sems.at[1])
    fetch_row = pltpu.make_async_copy(row_in, orders_row, sems.at[2])
    fetch_orders.start()
    fetch_row.start()
    fetch_harmonics.start()
    fetch_noise = pltpu.make_async_copy(noise_in, noise, sems.at[3])
    fetch_weights = pltpu.make_async_copy(weights_in, weights, sems.at[4])
    fetch_noise.start()
    fetch_weights.start()
    square = (SIDE, SIDE)
    alike = ((iota(square, 0) & 1) == (iota(square, 1) & 1)).astype(BF16)
    sel = (2 * CYCLES, 4 * ROWS)
    column = iota(sel, 1)
    in_half = (column >= 2 * ROWS).astype(jnp.int32)
    column = column - 2 * ROWS * in_half
    odd = (column >= ROWS).astype(jnp.int32)
    picked[...] = selection(iota(sel, 0) >> 1, odd == 1, in_half, column - ROWS * odd).astype(BF16)
    shape = (ROWS, SIDE)
    row, half = iota(shape, 0), iota(shape, 1) & 1
    held = slot_cycle(half, row)
    z = jnp.where(held >= 0, 4.0 * (64.0 - 2.0 * held.astype(F32)) / (3.0 * NPIX), 0.0)
    below_one = 1.0 - (1.0 - z * z)
    log_term = -below_one * (1.0 + below_one * (0.5 + below_one * (1.0 / 3.0)))
    fetch_orders.wait()
    order = orders[ma]
    order_out[...] = jnp.full(order_out.shape, order, jnp.int32)
    order_value = order.astype(F32)
    square = (SIDE, SIDE)
    lane, step = iota(square, 1), iota(square, 0)
    degree_index = (lane >> 1) * SIDE + step
    j = degree_index.astype(F32)
    degree = order_value + j
    alpha = jnp.sqrt(
        jnp.maximum((2.0 * degree - 1.0) * (2.0 * degree + 1.0), 0.0)
        / jnp.maximum(j * (j + 2.0 * order_value), 1.0)
    )
    beta = jnp.sqrt(
        jnp.maximum((j - 1.0) * (j - 1.0 + 2.0 * order_value), 0.0)
        / jnp.maximum((2.0 * degree - 3.0) * (2.0 * degree - 1.0), 1.0)
    )
    moving = degree_index > 0
    first[...] = jnp.where(moving, alpha, 0.0)
    second[...] = jnp.where(moving, -alpha * beta, 1.0)
    full = jnp.full(shape, order_value, F32)
    seed = jnp.exp(
        0.5 * jnp.log((2.0 * full + 1.0) / (4.0 * math.pi))
        - 0.25 * jnp.log(math.pi * (full + 0.25))
        + 0.5 * full * log_term
    )

    unroll = 16

    def compose(block, state):
        pu, pl_, qu, ql = state
        for s in range(unroll):
            i = block * unroll + s
            zc = z * first[pl.ds(i, 1), :]
            c2 = second[pl.ds(i, 1), :]
            pu, pl_ = zc * pu + c2 * pl_, pu
            qu, ql = zc * qu + c2 * ql, qu
        return pu, pl_, qu, ql

    fetch_row.wait()
    make_basis(orders_row, turns, basis, basis_turned, small_out)
    ones, zeros = jnp.ones(shape, F32), jnp.zeros(shape, F32)
    a, c, b, d = lax.fori_loop(0, SIDE // unroll, compose, (ones, zeros, zeros, ones))
    lanes = iota(shape, 1)
    for by in (2, 4, 8, 16, 32, 64):
        inside = lanes >= by
        ea = jnp.where(inside, pltpu.roll(a, by, 1), 1.0)
        eb = jnp.where(inside, pltpu.roll(b, by, 1), 0.0)
        ec = jnp.where(inside, pltpu.roll(c, by, 1), 0.0)
        ed = jnp.where(inside, pltpu.roll(d, by, 1), 1.0)
        a, b, c, d = a * ea + b * ec, a * eb + b * ed, c * ea + d * ec, c * eb + d * ed
    started = lanes >= 2
    upper = jnp.where(started, pltpu.roll(b, 2, 1) * seed, 0.0)
    lower = jnp.where(started, pltpu.roll(d, 2, 1) * seed, seed)

    fetch_harmonics.wait()
    valid = degree_index < LMAX - order
    even_lane = (lane & 1) == 0
    for r in range(2):
        turned = harmonics[r].T
        real = jnp.where(even_lane, turned, pltpu.roll(turned, 1, 1))
        imag = jnp.where(even_lane, pltpu.roll(turned, SIDE - 1, 1), turned)
        coefficients[2 * r] = jnp.where(valid, real, 0.0)
        coefficients[2 * r + 1] = jnp.where(valid, imag, 0.0)

    def advance(block, state):
        upper, lower, sums = state[0], state[1], list(state[2:])
        for s in range(unroll):
            i = block * unroll + s
            zc = z * first[pl.ds(i, 1), :]
            upper, lower = zc * upper + second[pl.ds(i, 1), :] * lower, upper
            table[i] = upper
            for f in range(4):
                at = 4 * (s % 2) + f
                sums[at] = sums[at] + coefficients[f, pl.ds(i, 1), :] * upper
        return (upper, lower, *sums)

    state = lax.fori_loop(0, SIDE // unroll, advance, (upper, lower) + (zeros,) * 8)
    sums = state[2:]
    high, low = split(jnp.concatenate(sums, axis=0))
    sums = mxu(jnp.concatenate([high, low], axis=1), jnp.concatenate([alike, alike], axis=0))
    small = (2 * ROWS, SIDE)
    pair, lane_half = iota(small, 1) >> 1, iota(small, 1) & 1
    held_sums = jnp.zeros(small, F32)
    for f in range(4):
        both = [sums[(4 * parity + f) * ROWS : (4 * parity + f + 1) * ROWS] for parity in range(2)]
        held_sums = jnp.where(pair == f, jnp.concatenate(both, axis=0), held_sums)
    halves = jnp.concatenate([jnp.where(lane_half == half, held_sums, 0.0) for half in range(2)], axis=0)
    high, low = split(halves)
    own = mxu(jnp.concatenate([picked[...], picked[...]], axis=1), jnp.concatenate([high, low], axis=0))
    even_lane = (iota(square, 1) & 1) == 0
    own = own + jnp.where(even_lane, pltpu.roll(own, SIDE - 1, 1), pltpu.roll(own, 1, 1))
    own = jnp.where(iota(square, 1) < 8, own, 0.0)
    before = pltpu.roll(own, 2, 0)
    after = pltpu.roll(own, 2 * CYCLES - 2, 0)
    sent[...] = own + pltpu.roll(before, 8, 1) + pltpu.roll(after, 16, 1)
    fetch_noise.wait()
    fetch_weights.wait()


def both_halves(pair, b):
    high, low = pair[:, :SIDE], pair[:, SIDE:]
    left = jnp.concatenate([jnp.concatenate([high, high], axis=1), jnp.concatenate([low, low], axis=1)], axis=0)
    product = mxu(left, jnp.concatenate(split(b), axis=0))
    return product[:SIDE] + product[SIDE:]


def row_pairs_swapped(x):
    even = (iota((SIDE, SIDE), 0) & 1) == 0
    return jnp.where(even, pltpu.roll(x, SIDE - 1, 0), pltpu.roll(x, 1, 0))


def euler_kernel(level_weights, turns, basis, basis_turned, small, received, noise, within, across, kappa_out, sent,
                 fields, counts, kappa, gradients, flips, sems):
    cycle = lax.axis_index("ma")
    parity = (cycle + 1 + NPIX // 4 - CYCLES // 2) % 2
    square = (SIDE, SIDE)
    lane, row = iota(square, 1), iota(square, 0)
    real_row = (row & 1) == 0
    a_cos, a_sin = turns[0], turns[1]
    spin_cos, spin_sin, weight = small[0], small[1], small[2]

    arrived = received[...]
    real_lane = ((lane >> 1) & 1) == 0
    partner = jnp.where(real_lane, pltpu.roll(arrived, SIDE - 2, 1), pltpu.roll(arrived, 2, 1))
    turned = (lane < 8) == (parity == 1)
    cs = jnp.where(turned, spin_cos, 1.0)
    sn = jnp.where(turned, spin_sin, 0.0)
    spun = weight * (arrived * cs + jnp.where(real_lane, -partner, partner) * sn)
    lefts = []
    for kk in range(3):
        for r in range(2):
            at = 8 * kk + 4 * r
            real = jnp.broadcast_to(spun[:, at : at + 1], square)
            imag = jnp.broadcast_to(spun[:, at + 2 : at + 3], square)
            lefts.append(jnp.where(real_row, real, -imag) * a_cos - jnp.where(real_row, imag, real) * a_sin)
    maps = both_halves(basis_turned[...], jnp.concatenate(lefts, axis=1))

    for r in range(2):
        for v in range(16):
            flips[r, pl.ds(v, 8, stride=16), :] = maps[8 * v : 8 * v + 8, r * SIDE : (r + 1) * SIDE]
        kappa[r] = flips[r].T
    keep_kappa = pltpu.make_async_copy(kappa, kappa_out, sems.at[0])
    keep_kappa.start()

    def arranged(x, slot):
        flips[slot] = x.T
        return jnp.concatenate([flips[slot, pl.ds(v, 8, stride=16), :] for v in range(16)], axis=0)

    own_noise = arranged(noise[...], 2)
    within_noise, across_noise = arranged(within[...], 3), arranged(across[...], 4)
    second_of_chip = cycle % 2 == 1
    noise_before = jnp.where(second_of_chip, within_noise, across_noise)
    noise_after = jnp.where(second_of_chip, across_noise, within_noise)
    sub = iota((8, SIDE), 0)

    def ratio(kk, r, weights):
        return 2.0 * (maps[:, (2 * kk + r) * SIDE : (2 * kk + r + 1) * SIDE] * weights)

    for r in range(2):
        here = ratio(0, r, own_noise)
        above = jnp.where(cycle > 0, ratio(1, r, noise_before), FAR)
        below = jnp.where(cycle < CYCLES - 1, ratio(2, r, noise_after), FAR)
        for n, x in enumerate((here, below, above)):
            fields[r, n, 8 : 8 + SIDE, :] = x
            last = pltpu.roll(x[SIDE - 8 :], 1, 0)
            fields[r, n, :8, :] = jnp.where(sub == 0, pltpu.roll(last, 1, 1), last)
            first = pltpu.roll(x[:8], 7, 0)
            fields[r, n, 8 + SIDE :, :] = jnp.where(sub == 7, pltpu.roll(first, SIDE - 1, 1), first)
    gradients[...] = jnp.zeros_like(gradients)

    def levels(r, group, odd, top):
        held = range(GROUP)
        number = [group * GROUP + g for g in held]
        twice = [t.astype(F32) * (12.0 / (LEVELS - 1)) - 6.0 for t in number]
        given = [level_weights[r, t] for t in number]
        known = {}

        def soft(n, v):
            if (n, v) not in known:
                x = fields[r, n, 8 * v + 8 : 8 * v + 16, :]
                known[n, v] = [jnp.tanh(x - twice[g]) for g in held]
            return known[n, v]

        totals = [jnp.zeros((8, SIDE), F32)] * GROUP
        for v in range(16):
            ahead, behind = (v + 1, v - 1) if odd else (v - 1, v + 1)
            slope = None
            for g in held:
                u, e, w, d = soft(0, v)[g], soft(0, ahead)[g], soft(0, behind)[g], soft(1, v)[g]
                n1 = -1.0 if top else soft(2, v)[g]
                down = soft(1, ahead)[g] * (d + e)
                up = 1.0 - e if top else soft(2, ahead)[g] * (e + n1)
                inner = down + up + w * (d + n1) - 2.0
                part = inner * (given[g] - (given[g] * u) * u)
                slope = part if slope is None else slope + part
                totals[g] = totals[g] + (u * (2.0 - down - up) if top else u * (2.0 - down))
            gradients[r, 8 * v : 8 * v + 8, :] += slope
        for g in held:
            counts[r * LEVELS + number[g]] = totals[g]

    def sweep(odd, top):
        def step(group, carry):
            for r in range(2):
                levels(r, group, odd, top)
            return carry

        lax.fori_loop(0, LEVELS // GROUP, step, 0)

    pl.when(cycle == 0)(lambda: sweep(True, True))
    pl.when((cycle > 0) & (parity == 1))(lambda: sweep(True, False))
    pl.when(parity == 0)(lambda: sweep(False, False))

    scale = 1.0 / (4.0 * math.sqrt(CYCLES * NPIX))
    back = both_halves(basis[...], jnp.concatenate([gradients[r] * (own_noise * scale) for r in range(2)], axis=1))
    pieces = []
    for r in range(2):
        sums = back[:, r * SIDE : (r + 1) * SIDE]
        pieces += [sums * a_cos, sums * a_sin]
    high, low = split(jnp.concatenate(pieces, axis=1))
    piece, to = iota((4 * SIDE, SIDE), 0) >> 7, iota((4 * SIDE, SIDE), 1)
    gather = (to == (piece >> 1) + 2 * (piece & 1)).astype(BF16)
    near = mxu(high, gather) + mxu(low, gather)
    far = pltpu.roll(row_pairs_swapped(near), SIDE - 2, 1)
    both = near + jnp.where(real_row, -far, far)
    other = row_pairs_swapped(both)
    cs = jnp.where(parity == 1, spin_cos, 1.0)
    sn = jnp.where(parity == 1, spin_sin, 0.0)
    dual = weight * jnp.where(real_row, both * cs - other * sn, -(both * cs + other * sn))
    stacked = jnp.where(lane < 2, dual, 0.0)
    level_sums = jnp.sum(counts[...], axis=1) * -0.125
    level_sums = level_sums + jnp.where(cycle == 0, 2.0 * NPIX / 8.0 / SIDE, 0.0)
    padded = jnp.concatenate([jnp.zeros_like(level_sums), level_sums], axis=0)
    level_row = dot(jnp.ones((8, SIDE), F32), padded, (1, 1))[:1]
    sent[...] = stacked + level_row
    keep_kappa.wait()


def adjoint_kernel(order_rows, received, table, gradient, turned):
    order = order_rows[:1]
    square = (SIDE, SIDE)
    lane, row = iota(square, 1), iota(square, 0)
    arrived = jnp.where(lane < CYCLES, received[...], 0.0)
    real = (row & 1) == 0
    pairs = jnp.where(real, arrived, 0.0) + pltpu.roll(jnp.where(real, 0.0, arrived), 2, 1)
    sel = (4 * ROWS, SIDE)
    at_row = iota(sel, 0)
    odd = (at_row >= 2 * ROWS).astype(jnp.int32)
    at_row = at_row - 2 * ROWS * odd
    in_half = (at_row >= ROWS).astype(jnp.int32)
    pick = selection(iota(sel, 1) >> 1, odd == 1, in_half, at_row - ROWS * in_half).astype(BF16)
    duals = mxu(jnp.concatenate([pick, pick], axis=1), jnp.concatenate(split(pairs), axis=0))
    even = (iota((ROWS, SIDE), 1) & 1) == 0

    def column(parity, half, r, c):
        start = (2 * parity + half) * ROWS
        at = 2 * c + r
        return jnp.broadcast_to(duals[start : start + ROWS, at : at + 1], (ROWS, SIDE))

    factors = [
        [
            (
                jnp.where(even, column(parity, 0, r, 0), column(parity, 1, r, 1)),
                jnp.where(even, column(parity, 0, r, 1), column(parity, 1, r, 0)),
            )
            for r in range(2)
        ]
        for parity in range(2)
    ]

    sub = iota((8, SIDE), 0)

    def merge(a, b, by):
        mine = (sub & by) == 0
        return jnp.where(mine, a, b) + pltpu.roll(jnp.where(mine, b, a), 8 - by, 0)

    even_lane = (iota((8, SIDE), 1) & 1) == 0

    def block(index):
        at = pl.ds(pl.multiple_of(index * 8, 8), 8)
        held = {}
        for s in range(8):
            value = table[index * 8 + s]
            for r in range(2):
                for kind in range(2):
                    product = value * factors[s % 2][r][kind]
                    part = product[:8] + product[8:16] + product[16:]
                    by = 1
                    while s & by:
                        part = merge(held.pop((r, kind, by)), part, by)
                        by *= 2
                    held[r, kind, by] = part
        for r in range(2):
            straight, crossed = held[r, 0, 8], held[r, 1, 8]
            crossed = jnp.where(even_lane, pltpu.roll(crossed, SIDE - 1, 1), pltpu.roll(crossed, 1, 1))
            turned[r, at, :] = straight + crossed

    def blocks(index, carry):
        for more in range(4):
            block(index * 4 + more)
        return carry

    lax.fori_loop(0, SIDE // 8 // 4, blocks, 0)
    for r in range(2):
        degree_index = (row >> 1) * SIDE + lane
        gradient[r] = jnp.where(degree_index < LMAX - order, turned[r].T, 0.0)


VMEM = pl.BlockSpec(memory_space=pltpu.VMEM)
SMEM = pl.BlockSpec(memory_space=pltpu.SMEM)
HBM = pl.BlockSpec(memory_space=pltpu.HBM)
PARAMS = pltpu.CompilerParams(vmem_limit_bytes=40 * 1024 * 1024)


def shards(harmonics, noise_weight, order_table, curve_weight):
    ta_count = lax.axis_size("ta")
    ma_count = lax.axis_size("ma")
    noise = noise_weight.reshape(SIDE, SIDE)
    within = lax.ppermute(noise, "ma", [(i, i ^ 1) for i in range(ma_count)])
    across = lax.ppermute(noise, "ma", [(i, i + 1 if i % 2 else i - 1) for i in range(1, ma_count - 1)])
    packed = harmonics.reshape(2, 2, 64, SIDE).transpose(0, 2, 1, 3).reshape(2, SIDE, SIDE)
    square = jax.ShapeDtypeStruct((2 * CYCLES, SIDE), F32)
    orders_there = pltpu.with_memory_space_constraint(order_table, pltpu.HBM)
    packed = pltpu.with_memory_space_constraint(packed, pltpu.HBM)
    table, sent, order_rows, turns, basis, basis_turned, small, noise_here, weights = pl.pallas_call(
        legendre_kernel,
        in_specs=[HBM] * 5,
        out_specs=[VMEM] * 9,
        out_shape=[
            jax.ShapeDtypeStruct((SIDE, ROWS, SIDE), F32),
            square,
            jax.ShapeDtypeStruct((8, SIDE), jnp.int32),
            jax.ShapeDtypeStruct((2, SIDE, SIDE), F32),
            jax.ShapeDtypeStruct((SIDE, 2 * SIDE), BF16),
            jax.ShapeDtypeStruct((SIDE, 2 * SIDE), BF16),
            jax.ShapeDtypeStruct((3, SIDE, SIDE), F32),
            jax.ShapeDtypeStruct((SIDE, SIDE), F32),
            jax.ShapeDtypeStruct((2, LEVELS), F32),
        ],
        scratch_shapes=[
            pltpu.VMEM((SIDE, SIDE), F32),
            pltpu.VMEM((SIDE, SIDE), F32),
            pltpu.VMEM((4, SIDE, SIDE), F32),
            pltpu.SMEM((CYCLES,), jnp.int32),
            pltpu.VMEM((2, SIDE, SIDE), F32),
            pltpu.VMEM((1, CYCLES), jnp.int32),
            pltpu.VMEM((2 * CYCLES, 4 * ROWS), BF16),
            pltpu.SemaphoreType.DMA((5,)),
        ],
        compiler_params=PARAMS,
        name="legendre",
    )(
        orders_there,
        pltpu.with_memory_space_constraint(order_table.reshape(1, CYCLES), pltpu.HBM),
        packed,
        pltpu.with_memory_space_constraint(noise, pltpu.HBM),
        pltpu.with_memory_space_constraint(curve_weight, pltpu.HBM),
    )
    sent, within, across = lax.optimization_barrier((sent, within, across))
    received = lax.all_to_all(sent, "ma", split_axis=0, concat_axis=0, tiled=True)
    kappa, sent = pl.pallas_call(
        euler_kernel,
        in_specs=[SMEM] + [VMEM] * 8,
        out_specs=[HBM, VMEM],
        out_shape=[jax.ShapeDtypeStruct((2, SIDE, SIDE), F32), square],
        scratch_shapes=[
            pltpu.VMEM((2, 3, SIDE + 16, SIDE), F32),
            pltpu.VMEM((2 * LEVELS, 8, SIDE), F32),
            pltpu.VMEM((2, SIDE, SIDE), F32),
            pltpu.VMEM((2, SIDE, SIDE), F32),
            pltpu.VMEM((5, SIDE, SIDE), F32),
            pltpu.SemaphoreType.DMA((1,)),
        ],
        compiler_params=PARAMS,
        name="euler",
    )(
        weights,
        turns,
        basis,
        basis_turned,
        small,
        received,
        noise_here,
        within,
        across,
    )
    received = lax.all_to_all(sent, "ma", split_axis=0, concat_axis=0, tiled=True)
    counts = jnp.sum(received.reshape(CYCLES, 2, SIDE)[:, 0, CYCLES:], axis=0).reshape(2, LEVELS)
    one, two, three = [lax.ppermute(counts, "ta", [(i, i ^ by) for i in range(ta_count)]) for by in (1, 2, 3)]
    curve = ((counts + one) + (two + three)) / (ta_count * CYCLES * NPIX)
    gradient = pl.pallas_call(
        adjoint_kernel,
        in_specs=[VMEM, VMEM, VMEM],
        out_specs=VMEM,
        out_shape=jax.ShapeDtypeStruct((2, SIDE, SIDE), F32),
        scratch_shapes=[pltpu.VMEM((2, SIDE, SIDE), F32)],
        compiler_params=PARAMS,
        name="adjoint",
    )(order_rows, received, table)
    gradient = gradient.reshape(2, 64, 2, SIDE).transpose(0, 2, 1, 3).reshape(1, 2, 1, 2, LMAX)
    return kappa.reshape(1, 2, 1, NPIX), curve, gradient


def solution(mesh):
    in_specs = (P("ta", None, "ma", None, None), P("ta", "ma", None), P(), P())
    out_specs = (P("ta", None, "ma", None), P(), P("ta", None, "ma", None, None))
    return jax.shard_map(shards, mesh=mesh, in_specs=in_specs, out_specs=out_specs, check_vma=False)
```

```python
import math

import jax
import jax.numpy as jnp
from jax import lax
from jax.experimental import pallas as pl
from jax.experimental.pallas import tpu as pltpu
from jax.sharding import PartitionSpec as P

F32 = jnp.float32
BF16 = jnp.bfloat16
HIGHEST = lax.Precision.HIGHEST
NPIX = 16384
LMAX = 8192
CYCLES = 64
LEVELS = 32
SIDE = 128
ROWS = 24
GROUP = 4
FAR = -1.0e9


def iota(shape, dim):
    return lax.broadcasted_iota(jnp.int32, shape, dim)


def dot(a, b, contract):
    return lax.dot_general(a, b, ((contract[:1], contract[1:]), ((), ())), precision=HIGHEST,
                           preferred_element_type=F32)


def slot_cycle(half, row):
    own = jnp.where(row < 16, row + 16 * half, -1)
    return jnp.where((row == 16) & (half == 0), 32, own)


def selection(cycle, odd, half, row):
    mirrored = jnp.where(cycle > 32, 64 - cycle, cycle)
    sign = jnp.where((cycle > 32) & odd, -1.0, 1.0)
    return jnp.where(slot_cycle(half, row) == mirrored, sign, 0.0).astype(F32)


def split(x):
    high = x.astype(BF16)
    return high, (x - high.astype(F32)).astype(BF16)


def mxu(a, b):
    return lax.dot_general(a, b, (((1,), (0,)), ((), ())), preferred_element_type=F32)


def turn_cos_sin(index, whole):
    quarter = whole // 4
    index = index & (whole - 1)
    quadrant = (index + quarter // 2) >> (quarter.bit_length() - 1)
    x = (index - quadrant * quarter).astype(F32) * (2.0 * math.pi / whole)
    y = x * x
    sine = x * (1.0 + y * (-1.0 / 6 + y * (1.0 / 120 + y * (-1.0 / 5040 + y * (1.0 / 362880)))))
    cosine = 1.0 + y * (-0.5 + y * (1.0 / 24 + y * (-1.0 / 720 + y * (1.0 / 40320 - y * (1.0 / 3628800)))))
    swap = (quadrant & 1) == 1
    c = jnp.where(swap, sine, cosine)
    s = jnp.where(swap, cosine, sine)
    c = jnp.where(((quadrant + 1) & 2) == 2, -c, c)
    s = jnp.where((quadrant & 2) == 2, -s, s)
    return c, s


def make_basis(orders_row, turns, basis, basis_turned, small):
    square = (SIDE, SIDE)
    lane, row = iota(square, 1), iota(square, 0)
    twice = (iota((CYCLES, SIDE), 1) >> 1) == iota((CYCLES, SIDE), 0)
    eight = jnp.broadcast_to(orders_row[...].astype(F32), (8, CYCLES))
    eight = dot(eight, twice.astype(F32), (1, 0)).astype(jnp.int32)
    orders = jnp.broadcast_to(eight[:1], square)
    down = orders.astype(F32).T.astype(jnp.int32)
    turns[0], turns[1] = turn_cos_sin(down * lane, SIDE)
    pixel = 16 * (row & 7) + (row >> 3)
    cosine, sine = turn_cos_sin(orders * pixel, NPIX)
    turned = jnp.where((lane & 1) == 0, cosine, sine)
    for ref, value in ((basis, turned.T), (basis_turned, turned)):
        ref[:, :SIDE], ref[:, SIDE:] = split(value)
    small[0], small[1] = turn_cos_sin(down, 2 * NPIX)
    small[2] = jnp.where(down == 0, 1.0, 2.0)


def legendre_kernel(orders_in, row_in, harmonics_in, noise_in, weights_in, table, sent, order_out, turns, basis, basis_turned,
                    small_out, noise, weights,
                    first, second, coefficients, orders, harmonics, orders_row, picked, sems):
    ma = lax.axis_index("ma")
    fetch_orders = pltpu.make_async_copy(orders_in, orders, sems.at[0])
    fetch_harmonics = pltpu.make_async_copy(harmonics_in, harmonics, sems.at[1])
    fetch_row = pltpu.make_async_copy(row_in, orders_row, sems.at[2])
    fetch_orders.start()
    fetch_row.start()
    fetch_harmonics.start()
    fetch_noise = pltpu.make_async_copy(noise_in, noise, sems.at[3])
    fetch_weights = pltpu.make_async_copy(weights_in, weights, sems.at[4])
    fetch_noise.start()
    fetch_weights.start()
    square = (SIDE, SIDE)
    alike = ((iota(square, 0) & 1) == (iota(square, 1) & 1)).astype(BF16)
    sel = (2 * CYCLES, 4 * ROWS)
    column = iota(sel, 1)
    in_half = (column >= 2 * ROWS).astype(jnp.int32)
    column = column - 2 * ROWS * in_half
    odd = (column >= ROWS).astype(jnp.int32)
    picked[...] = selection(iota(sel, 0) >> 1, odd == 1, in_half, column - ROWS * odd).astype(BF16)
    shape = (ROWS, SIDE)
    row, half = iota(shape, 0), iota(shape, 1) & 1
    held = slot_cycle(half, row)
    z = jnp.where(held >= 0, 4.0 * (64.0 - 2.0 * held.astype(F32)) / (3.0 * NPIX), 0.0)
    below_one = 1.0 - (1.0 - z * z)
    log_term = -below_one * (1.0 + below_one * (0.5 + below_one * (1.0 / 3.0)))
    fetch_orders.wait()
    order = orders[ma]
    order_out[...] = jnp.full(order_out.shape, order, jnp.int32)
    order_value = order.astype(F32)
    square = (SIDE, SIDE)
    lane, step = iota(square, 1), iota(square, 0)
    degree_index = (lane >> 1) * SIDE + step
    j = degree_index.astype(F32)
    degree = order_value + j
    alpha = jnp.sqrt(
        jnp.maximum((2.0 * degree - 1.0) * (2.0 * degree + 1.0), 0.0)
        / jnp.maximum(j * (j + 2.0 * order_value), 1.0)
    )
    beta = jnp.sqrt(
        jnp.maximum((j - 1.0) * (j - 1.0 + 2.0 * order_value), 0.0)
        / jnp.maximum((2.0 * degree - 3.0) * (2.0 * degree - 1.0), 1.0)
    )
    moving = degree_index > 0
    first[...] = jnp.where(moving, alpha, 0.0)
    second[...] = jnp.where(moving, -alpha * beta, 1.0)
    full = jnp.full(shape, order_value, F32)
    seed = jnp.exp(
        0.5 * jnp.log((2.0 * full + 1.0) / (4.0 * math.pi))
        - 0.25 * jnp.log(math.pi * (full + 0.25))
        + 0.5 * full * log_term
    )

    unroll = 16

    def compose(block, state):
        pu, pl_, qu, ql = state
        for s in range(unroll):
            i = block * unroll + s
            zc = z * first[pl.ds(i, 1), :]
            c2 = second[pl.ds(i, 1), :]
            pu, pl_ = zc * pu + c2 * pl_, pu
            qu, ql = zc * qu + c2 * ql, qu
        return pu, pl_, qu, ql

    fetch_row.wait()
    make_basis(orders_row, turns, basis, basis_turned, small_out)
    ones, zeros = jnp.ones(shape, F32), jnp.zeros(shape, F32)
    a, c, b, d = lax.fori_loop(0, SIDE // unroll, compose, (ones, zeros, zeros, ones))
    lanes = iota(shape, 1)
    for by in (2, 4, 8, 16, 32, 64):
        inside = lanes >= by
        ea = jnp.where(inside, pltpu.roll(a, by, 1), 1.0)
        eb = jnp.where(inside, pltpu.roll(b, by, 1), 0.0)
        ec = jnp.where(inside, pltpu.roll(c, by, 1), 0.0)
        ed = jnp.where(inside, pltpu.roll(d, by, 1), 1.0)
        a, b, c, d = a * ea + b * ec, a * eb + b * ed, c * ea + d * ec, c * eb + d * ed
    started = lanes >= 2
    upper = jnp.where(started, pltpu.roll(b, 2, 1) * seed, 0.0)
    lower = jnp.where(started, pltpu.roll(d, 2, 1) * seed, seed)

    fetch_harmonics.wait()
    valid = degree_index < LMAX - order
    even_lane = (lane & 1) == 0
    for r in range(2):
        turned = harmonics[r].T
        real = jnp.where(even_lane, turned, pltpu.roll(turned, 1, 1))
        imag = jnp.where(even_lane, pltpu.roll(turned, SIDE - 1, 1), turned)
        coefficients[2 * r] = jnp.where(valid, real, 0.0)
        coefficients[2 * r + 1] = jnp.where(valid, imag, 0.0)

    def advance(block, state):
        upper, lower, sums = state[0], state[1], list(state[2:])
        for s in range(unroll):
            i = block * unroll + s
            zc = z * first[pl.ds(i, 1), :]
            upper, lower = zc * upper + second[pl.ds(i, 1), :] * lower, upper
            table[i] = upper
            for f in range(4):
                at = 4 * (s % 2) + f
                sums[at] = sums[at] + coefficients[f, pl.ds(i, 1), :] * upper
        return (upper, lower, *sums)

    state = lax.fori_loop(0, SIDE // unroll, advance, (upper, lower) + (zeros,) * 8)
    sums = state[2:]
    high, low = split(jnp.concatenate(sums, axis=0))
    sums = mxu(jnp.concatenate([high, low], axis=1), jnp.concatenate([alike, alike], axis=0))
    small = (2 * ROWS, SIDE)
    pair, lane_half = iota(small, 1) >> 1, iota(small, 1) & 1
    held_sums = jnp.zeros(small, F32)
    for f in range(4):
        both = [sums[(4 * parity + f) * ROWS : (4 * parity + f + 1) * ROWS] for parity in range(2)]
        held_sums = jnp.where(pair == f, jnp.concatenate(both, axis=0), held_sums)
    halves = jnp.concatenate([jnp.where(lane_half == half, held_sums, 0.0) for half in range(2)], axis=0)
    high, low = split(halves)
    own = mxu(jnp.concatenate([picked[...], picked[...]], axis=1), jnp.concatenate([high, low], axis=0))
    even_lane = (iota(square, 1) & 1) == 0
    own = own + jnp.where(even_lane, pltpu.roll(own, SIDE - 1, 1), pltpu.roll(own, 1, 1))
    own = jnp.where(iota(square, 1) < 8, own, 0.0)
    before = pltpu.roll(own, 2, 0)
    after = pltpu.roll(own, 2 * CYCLES - 2, 0)
    sent[...] = own + pltpu.roll(before, 8, 1) + pltpu.roll(after, 16, 1)
    fetch_noise.wait()
    fetch_weights.wait()


def both_halves(pair, b):
    high, low = pair[:, :SIDE], pair[:, SIDE:]
    left = jnp.concatenate([jnp.concatenate([high, high], axis=1), jnp.concatenate([low, low], axis=1)], axis=0)
    product = mxu(left, jnp.concatenate(split(b), axis=0))
    return product[:SIDE] + product[SIDE:]


def row_pairs_swapped(x):
    even = (iota((SIDE, SIDE), 0) & 1) == 0
    return jnp.where(even, pltpu.roll(x, SIDE - 1, 0), pltpu.roll(x, 1, 0))


def euler_kernel(level_weights, turns, basis, basis_turned, small, received, noise, within, across, kappa_out, sent,
                 fields, counts, kappa, gradients, flips, sems):
    cycle = lax.axis_index("ma")
    parity = (cycle + 1 + NPIX // 4 - CYCLES // 2) % 2
    square = (SIDE, SIDE)
    lane, row = iota(square, 1), iota(square, 0)
    real_row = (row & 1) == 0
    a_cos, a_sin = turns[0], turns[1]
    spin_cos, spin_sin, weight = small[0], small[1], small[2]

    arrived = received[...]
    real_lane = ((lane >> 1) & 1) == 0
    partner = jnp.where(real_lane, pltpu.roll(arrived, SIDE - 2, 1), pltpu.roll(arrived, 2, 1))
    turned = (lane < 8) == (parity == 1)
    cs = jnp.where(turned, spin_cos, 1.0)
    sn = jnp.where(turned, spin_sin, 0.0)
    spun = weight * (arrived * cs + jnp.where(real_lane, -partner, partner) * sn)
    lefts = []
    for kk in range(3):
        for r in range(2):
            at = 8 * kk + 4 * r
            real = jnp.broadcast_to(spun[:, at : at + 1], square)
            imag = jnp.broadcast_to(spun[:, at + 2 : at + 3], square)
            lefts.append(jnp.where(real_row, real, -imag) * a_cos - jnp.where(real_row, imag, real) * a_sin)
    maps = both_halves(basis_turned[...], jnp.concatenate(lefts, axis=1))

    for r in range(2):
        for v in range(16):
            flips[r, pl.ds(v, 8, stride=16), :] = maps[8 * v : 8 * v + 8, r * SIDE : (r + 1) * SIDE]
        kappa[r] = flips[r].T
    keep_kappa = pltpu.make_async_copy(kappa, kappa_out, sems.at[0])
    keep_kappa.start()

    def arranged(x, slot):
        flips[slot] = x.T
        return jnp.concatenate([flips[slot, pl.ds(v, 8, stride=16), :] for v in range(16)], axis=0)

    own_noise = arranged(noise[...], 2)
    within_noise, across_noise = arranged(within[...], 3), arranged(across[...], 4)
    second_of_chip = cycle % 2 == 1
    noise_before = jnp.where(second_of_chip, within_noise, across_noise)
    noise_after = jnp.where(second_of_chip, across_noise, within_noise)
    sub = iota((8, SIDE), 0)

    def ratio(kk, r, weights):
        return 2.0 * (maps[:, (2 * kk + r) * SIDE : (2 * kk + r + 1) * SIDE] * weights)

    for r in range(2):
        here = ratio(0, r, own_noise)
        above = jnp.where(cycle > 0, ratio(1, r, noise_before), FAR)
        below = jnp.where(cycle < CYCLES - 1, ratio(2, r, noise_after), FAR)
        for n, x in enumerate((here, below, above)):
            fields[r, n, 8 : 8 + SIDE, :] = x
            last = pltpu.roll(x[SIDE - 8 :], 1, 0)
            fields[r, n, :8, :] = jnp.where(sub == 0, pltpu.roll(last, 1, 1), last)
            first = pltpu.roll(x[:8], 7, 0)
            fields[r, n, 8 + SIDE :, :] = jnp.where(sub == 7, pltpu.roll(first, SIDE - 1, 1), first)
    gradients[...] = jnp.zeros_like(gradients)

    def levels(r, group, odd, top):
        held = range(GROUP)
        number = [group * GROUP + g for g in held]
        twice = [t.astype(F32) * (12.0 / (LEVELS - 1)) - 6.0 for t in number]
        given = [level_weights[r, t] for t in number]
        known = {}

        def soft(n, v):
            if (n, v) not in known:
                x = fields[r, n, 8 * v + 8 : 8 * v + 16, :]
                known[n, v] = [jnp.tanh(x - twice[g]) for g in held]
            return known[n, v]

        totals = [jnp.zeros((8, SIDE), F32)] * GROUP
        for v in range(16):
            ahead, behind = (v + 1, v - 1) if odd else (v - 1, v + 1)
            slope = None
            for g in held:
                u, e, w, d = soft(0, v)[g], soft(0, ahead)[g], soft(0, behind)[g], soft(1, v)[g]
                n1 = -1.0 if top else soft(2, v)[g]
                down = soft(1, ahead)[g] * (d + e)
                up = 1.0 - e if top else soft(2, ahead)[g] * (e + n1)
                inner = down + up + w * (d + n1) - 2.0
                part = inner * (given[g] - (given[g] * u) * u)
                slope = part if slope is None else slope + part
                totals[g] = totals[g] + (u * (2.0 - down - up) if top else u * (2.0 - down))
            gradients[r, 8 * v : 8 * v + 8, :] += slope
        for g in held:
            counts[r * LEVELS + number[g]] = totals[g]

    def sweep(odd, top):
        def step(group, carry):
            for r in range(2):
                levels(r, group, odd, top)
            return carry

        lax.fori_loop(0, LEVELS // GROUP, step, 0)

    pl.when(cycle == 0)(lambda: sweep(True, True))
    pl.when((cycle > 0) & (parity == 1))(lambda: sweep(True, False))
    pl.when(parity == 0)(lambda: sweep(False, False))

    scale = 1.0 / (4.0 * math.sqrt(CYCLES * NPIX))
    back = both_halves(basis[...], jnp.concatenate([gradients[r] * (own_noise * scale) for r in range(2)], axis=1))
    pieces = []
    for r in range(2):
        sums = back[:, r * SIDE : (r + 1) * SIDE]
        pieces += [sums * a_cos, sums * a_sin]
    high, low = split(jnp.concatenate(pieces, axis=1))
    piece, to = iota((4 * SIDE, SIDE), 0) >> 7, iota((4 * SIDE, SIDE), 1)
    gather = (to == (piece >> 1) + 2 * (piece & 1)).astype(BF16)
    near = mxu(high, gather) + mxu(low, gather)
    far = pltpu.roll(row_pairs_swapped(near), SIDE - 2, 1)
    both = near + jnp.where(real_row, -far, far)
    other = row_pairs_swapped(both)
    cs = jnp.where(parity == 1, spin_cos, 1.0)
    sn = jnp.where(parity == 1, spin_sin, 0.0)
    dual = weight * jnp.where(real_row, both * cs - other * sn, -(both * cs + other * sn))
    stacked = jnp.where(lane < 2, dual, 0.0)
    level_sums = jnp.sum(counts[...], axis=1) * -0.125
    level_sums = level_sums + jnp.where(cycle == 0, 2.0 * NPIX / 8.0 / SIDE, 0.0)
    padded = jnp.concatenate([jnp.zeros_like(level_sums), level_sums], axis=0)
    level_row = dot(jnp.ones((8, SIDE), F32), padded, (1, 1))[:1]
    sent[...] = stacked + level_row
    keep_kappa.wait()


def adjoint_kernel(order_rows, received, table, gradient, turned):
    order = order_rows[:1]
    square = (SIDE, SIDE)
    lane, row = iota(square, 1), iota(square, 0)
    arrived = jnp.where(lane < CYCLES, received[...], 0.0)
    real = (row & 1) == 0
    pairs = jnp.where(real, arrived, 0.0) + pltpu.roll(jnp.where(real, 0.0, arrived), 2, 1)
    sel = (4 * ROWS, SIDE)
    at_row = iota(sel, 0)
    odd = (at_row >= 2 * ROWS).astype(jnp.int32)
    at_row = at_row - 2 * ROWS * odd
    in_half = (at_row >= ROWS).astype(jnp.int32)
    pick = selection(iota(sel, 1) >> 1, odd == 1, in_half, at_row - ROWS * in_half).astype(BF16)
    duals = mxu(jnp.concatenate([pick, pick], axis=1), jnp.concatenate(split(pairs), axis=0))
    even = (iota((ROWS, SIDE), 1) & 1) == 0

    def column(parity, half, r, c):
        start = (2 * parity + half) * ROWS
        at = 2 * c + r
        return jnp.broadcast_to(duals[start : start + ROWS, at : at + 1], (ROWS, SIDE))

    factors = [
        [
            (
                jnp.where(even, column(parity, 0, r, 0), column(parity, 1, r, 1)),
                jnp.where(even, column(parity, 0, r, 1), column(parity, 1, r, 0)),
            )
            for r in range(2)
        ]
        for parity in range(2)
    ]

    sub = iota((8, SIDE), 0)

    def merge(a, b, by):
        mine = (sub & by) == 0
        return jnp.where(mine, a, b) + pltpu.roll(jnp.where(mine, b, a), 8 - by, 0)

    even_lane = (iota((8, SIDE), 1) & 1) == 0

    def block(index):
        at = pl.ds(pl.multiple_of(index * 8, 8), 8)
        held = {}
        for s in range(8):
            value = table[index * 8 + s]
            for r in range(2):
                for kind in range(2):
                    product = value * factors[s % 2][r][kind]
                    part = product[:8] + product[8:16] + product[16:]
                    by = 1
                    while s & by:
                        part = merge(held.pop((r, kind, by)), part, by)
                        by *= 2
                    held[r, kind, by] = part
        for r in range(2):
            straight, crossed = held[r, 0, 8], held[r, 1, 8]
            crossed = jnp.where(even_lane, pltpu.roll(crossed, SIDE - 1, 1), pltpu.roll(crossed, 1, 1))
            turned[r, at, :] = straight + crossed

    def blocks(index, carry):
        for more in range(4):
            block(index * 4 + more)
        return carry

    lax.fori_loop(0, SIDE // 8 // 4, blocks, 0)
    for r in range(2):
        degree_index = (row >> 1) * SIDE + lane
        gradient[r] = jnp.where(degree_index < LMAX - order, turned[r].T, 0.0)


VMEM = pl.BlockSpec(memory_space=pltpu.VMEM)
SMEM = pl.BlockSpec(memory_space=pltpu.SMEM)
HBM = pl.BlockSpec(memory_space=pltpu.HBM)
PARAMS = pltpu.CompilerParams(vmem_limit_bytes=40 * 1024 * 1024)


def shards(harmonics, noise_weight, order_table, curve_weight):
    ta_count = lax.axis_size("ta")
    ma_count = lax.axis_size("ma")
    noise = noise_weight.reshape(SIDE, SIDE)
    within = lax.ppermute(noise, "ma", [(i, i ^ 1) for i in range(ma_count)])
    across = lax.ppermute(noise, "ma", [(i, (i + (1 if i % 2 else -1)) % ma_count) for i in range(ma_count)])
    packed = harmonics.reshape(2, 2, 64, SIDE).transpose(0, 2, 1, 3).reshape(2, SIDE, SIDE)
    square = jax.ShapeDtypeStruct((2 * CYCLES, SIDE), F32)
    orders_there = pltpu.with_memory_space_constraint(order_table, pltpu.HBM)
    packed = pltpu.with_memory_space_constraint(packed, pltpu.HBM)
    table, sent, order_rows, turns, basis, basis_turned, small, noise_here, weights = pl.pallas_call(
        legendre_kernel,
        in_specs=[HBM] * 5,
        out_specs=[VMEM] * 9,
        out_shape=[
            jax.ShapeDtypeStruct((SIDE, ROWS, SIDE), F32),
            square,
            jax.ShapeDtypeStruct((8, SIDE), jnp.int32),
            jax.ShapeDtypeStruct((2, SIDE, SIDE), F32),
            jax.ShapeDtypeStruct((SIDE, 2 * SIDE), BF16),
            jax.ShapeDtypeStruct((SIDE, 2 * SIDE), BF16),
            jax.ShapeDtypeStruct((3, SIDE, SIDE), F32),
            jax.ShapeDtypeStruct((SIDE, SIDE), F32),
            jax.ShapeDtypeStruct((2, LEVELS), F32),
        ],
        scratch_shapes=[
            pltpu.VMEM((SIDE, SIDE), F32),
            pltpu.VMEM((SIDE, SIDE), F32),
            pltpu.VMEM((4, SIDE, SIDE), F32),
            pltpu.SMEM((CYCLES,), jnp.int32),
            pltpu.VMEM((2, SIDE, SIDE), F32),
            pltpu.VMEM((1, CYCLES), jnp.int32),
            pltpu.VMEM((2 * CYCLES, 4 * ROWS), BF16),
            pltpu.SemaphoreType.DMA((5,)),
        ],
        compiler_params=PARAMS,
        name="legendre",
    )(
        orders_there,
        pltpu.with_memory_space_constraint(order_table.reshape(1, CYCLES), pltpu.HBM),
        packed,
        pltpu.with_memory_space_constraint(noise, pltpu.HBM),
        pltpu.with_memory_space_constraint(curve_weight, pltpu.HBM),
    )
    sent, within, across = lax.optimization_barrier((sent, within, across))
    received = lax.all_to_all(sent, "ma", split_axis=0, concat_axis=0, tiled=True)
    kappa, sent = pl.pallas_call(
        euler_kernel,
        in_specs=[SMEM] + [VMEM] * 8,
        out_specs=[HBM, VMEM],
        out_shape=[jax.ShapeDtypeStruct((2, SIDE, SIDE), F32), square],
        scratch_shapes=[
            pltpu.VMEM((2, 3, SIDE + 16, SIDE), F32),
            pltpu.VMEM((2 * LEVELS, 8, SIDE), F32),
            pltpu.VMEM((2, SIDE, SIDE), F32),
            pltpu.VMEM((2, SIDE, SIDE), F32),
            pltpu.VMEM((5, SIDE, SIDE), F32),
            pltpu.SemaphoreType.DMA((1,)),
        ],
        compiler_params=PARAMS,
        name="euler",
    )(
        weights,
        turns,
        basis,
        basis_turned,
        small,
        received,
        noise_here,
        within,
        across,
    )
    received = lax.all_to_all(sent, "ma", split_axis=0, concat_axis=0, tiled=True)
    counts = jnp.sum(received.reshape(CYCLES, 2, SIDE)[:, 0, CYCLES:], axis=0).reshape(2, LEVELS)
    one, two, three = [lax.ppermute(counts, "ta", [(i, i ^ by) for i in range(ta_count)]) for by in (1, 2, 3)]
    curve = ((counts + one) + (two + three)) / (ta_count * CYCLES * NPIX)
    gradient = pl.pallas_call(
        adjoint_kernel,
        in_specs=[VMEM, VMEM, VMEM],
        out_specs=VMEM,
        out_shape=jax.ShapeDtypeStruct((2, SIDE, SIDE), F32),
        scratch_shapes=[pltpu.VMEM((2, SIDE, SIDE), F32)],
        compiler_params=PARAMS,
        name="adjoint",
    )(order_rows, received, table)
    gradient = gradient.reshape(2, 64, 2, SIDE).transpose(0, 2, 1, 3).reshape(1, 2, 1, 2, LMAX)
    return kappa.reshape(1, 2, 1, NPIX), curve, gradient


def solution(mesh):
    in_specs = (P("ta", None, "ma", None, None), P("ta", "ma", None), P(), P())
    out_specs = (P("ta", None, "ma", None), P(), P("ta", None, "ma", None, None))
    return jax.shard_map(shards, mesh=mesh, in_specs=in_specs, out_specs=out_specs, check_vma=False)
```

```python
import math

import jax
import jax.numpy as jnp
from jax import lax
from jax.experimental import pallas as pl
from jax.experimental.pallas import tpu as pltpu
from jax.sharding import PartitionSpec as P

F32 = jnp.float32
BF16 = jnp.bfloat16
HIGHEST = lax.Precision.HIGHEST
NPIX = 16384
LMAX = 8192
CYCLES = 64
LEVELS = 32
SIDE = 128
ROWS = 24
GROUP = 4
FAR = -1.0e9


def iota(shape, dim):
    return lax.broadcasted_iota(jnp.int32, shape, dim)


def dot(a, b, contract):
    return lax.dot_general(a, b, ((contract[:1], contract[1:]), ((), ())), precision=HIGHEST,
                           preferred_element_type=F32)


def slot_cycle(half, row):
    own = jnp.where(row < 16, row + 16 * half, -1)
    return jnp.where((row == 16) & (half == 0), 32, own)


def selection(cycle, odd, half, row):
    mirrored = jnp.where(cycle > 32, 64 - cycle, cycle)
    sign = jnp.where((cycle > 32) & odd, -1.0, 1.0)
    return jnp.where(slot_cycle(half, row) == mirrored, sign, 0.0).astype(F32)


def split(x):
    high = x.astype(BF16)
    return high, (x - high.astype(F32)).astype(BF16)


def mxu(a, b):
    return lax.dot_general(a, b, (((1,), (0,)), ((), ())), preferred_element_type=F32)


def turn_cos_sin(index, whole):
    quarter = whole // 4
    index = index & (whole - 1)
    quadrant = (index + quarter // 2) >> (quarter.bit_length() - 1)
    x = (index - quadrant * quarter).astype(F32) * (2.0 * math.pi / whole)
    y = x * x
    sine = x * (1.0 + y * (-1.0 / 6 + y * (1.0 / 120 + y * (-1.0 / 5040 + y * (1.0 / 362880)))))
    cosine = 1.0 + y * (-0.5 + y * (1.0 / 24 + y * (-1.0 / 720 + y * (1.0 / 40320 - y * (1.0 / 3628800)))))
    swap = (quadrant & 1) == 1
    c = jnp.where(swap, sine, cosine)
    s = jnp.where(swap, cosine, sine)
    c = jnp.where(((quadrant + 1) & 2) == 2, -c, c)
    s = jnp.where((quadrant & 2) == 2, -s, s)
    return c, s


def make_basis(orders_row, turns, basis, basis_turned, small):
    square = (SIDE, SIDE)
    lane, row = iota(square, 1), iota(square, 0)
    twice = (iota((CYCLES, SIDE), 1) >> 1) == iota((CYCLES, SIDE), 0)
    eight = jnp.broadcast_to(orders_row[...].astype(F32), (8, CYCLES))
    eight = dot(eight, twice.astype(F32), (1, 0)).astype(jnp.int32)
    orders = jnp.broadcast_to(eight[:1], square)
    down = orders.astype(F32).T.astype(jnp.int32)
    turns[0], turns[1] = turn_cos_sin(down * lane, SIDE)
    pixel = 16 * (row & 7) + (row >> 3)
    cosine, sine = turn_cos_sin(orders * pixel, NPIX)
    turned = jnp.where((lane & 1) == 0, cosine, sine)
    for ref, value in ((basis, turned.T), (basis_turned, turned)):
        ref[:, :SIDE], ref[:, SIDE:] = split(value)
    small[0], small[1] = turn_cos_sin(down, 2 * NPIX)
    small[2] = jnp.where(down == 0, 1.0, 2.0)


def legendre_kernel(orders_in, row_in, harmonics_in, noise_in, weights_in, table, sent, order_out, turns, basis, basis_turned,
                    small_out, noise, weights,
                    first, second, coefficients, orders, harmonics, orders_row, picked, sems):
    ma = lax.axis_index("ma")
    fetch_orders = pltpu.make_async_copy(orders_in, orders, sems.at[0])
    fetch_harmonics = pltpu.make_async_copy(harmonics_in, harmonics, sems.at[1])
    fetch_row = pltpu.make_async_copy(row_in, orders_row, sems.at[2])
    fetch_orders.start()
    fetch_row.start()
    fetch_harmonics.start()
    fetch_noise = pltpu.make_async_copy(noise_in, noise, sems.at[3])
    fetch_weights = pltpu.make_async_copy(weights_in, weights, sems.at[4])
    fetch_noise.start()
    fetch_weights.start()
    square = (SIDE, SIDE)
    alike = ((iota(square, 0) & 1) == (iota(square, 1) & 1)).astype(BF16)
    sel = (2 * CYCLES, 4 * ROWS)
    column = iota(sel, 1)
    in_half = (column >= 2 * ROWS).astype(jnp.int32)
    column = column - 2 * ROWS * in_half
    odd = (column >= ROWS).astype(jnp.int32)
    picked[...] = selection(iota(sel, 0) >> 1, odd == 1, in_half, column - ROWS * odd).astype(BF16)
    shape = (ROWS, SIDE)
    row, half = iota(shape, 0), iota(shape, 1) & 1
    held = slot_cycle(half, row)
    z = jnp.where(held >= 0, 4.0 * (64.0 - 2.0 * held.astype(F32)) / (3.0 * NPIX), 0.0)
    below_one = 1.0 - (1.0 - z * z)
    log_term = -below_one * (1.0 + below_one * (0.5 + below_one * (1.0 / 3.0)))
    fetch_orders.wait()
    order = orders[ma]
    order_out[...] = jnp.full(order_out.shape, order, jnp.int32)
    order_value = order.astype(F32)
    square = (SIDE, SIDE)
    lane, step = iota(square, 1), iota(square, 0)
    degree_index = (lane >> 1) * SIDE + step
    j = degree_index.astype(F32)
    degree = order_value + j
    alpha = jnp.sqrt(
        jnp.maximum((2.0 * degree - 1.0) * (2.0 * degree + 1.0), 0.0)
        / jnp.maximum(j * (j + 2.0 * order_value), 1.0)
    )
    beta = jnp.sqrt(
        jnp.maximum((j - 1.0) * (j - 1.0 + 2.0 * order_value), 0.0)
        / jnp.maximum((2.0 * degree - 3.0) * (2.0 * degree - 1.0), 1.0)
    )
    moving = degree_index > 0
    first[...] = jnp.where(moving, alpha, 0.0)
    second[...] = jnp.where(moving, -alpha * beta, 1.0)
    full = jnp.full(shape, order_value, F32)
    seed = jnp.exp(
        0.5 * jnp.log((2.0 * full + 1.0) / (4.0 * math.pi))
        - 0.25 * jnp.log(math.pi * (full + 0.25))
        + 0.5 * full * log_term
    )

    unroll = 16

    def compose(block, state):
        pu, pl_, qu, ql = state
        for s in range(unroll):
            i = block * unroll + s
            zc = z * first[pl.ds(i, 1), :]
            c2 = second[pl.ds(i, 1), :]
            pu, pl_ = zc * pu + c2 * pl_, pu
            qu, ql = zc * qu + c2 * ql, qu
        return pu, pl_, qu, ql

    fetch_row.wait()
    make_basis(orders_row, turns, basis, basis_turned, small_out)
    ones, zeros = jnp.ones(shape, F32), jnp.zeros(shape, F32)
    a, c, b, d = lax.fori_loop(0, SIDE // unroll, compose, (ones, zeros, zeros, ones))
    lanes = iota(shape, 1)
    for by in (2, 4, 8, 16, 32, 64):
        inside = lanes >= by
        ea = jnp.where(inside, pltpu.roll(a, by, 1), 1.0)
        eb = jnp.where(inside, pltpu.roll(b, by, 1), 0.0)
        ec = jnp.where(inside, pltpu.roll(c, by, 1), 0.0)
        ed = jnp.where(inside, pltpu.roll(d, by, 1), 1.0)
        a, b, c, d = a * ea + b * ec, a * eb + b * ed, c * ea + d * ec, c * eb + d * ed
    started = lanes >= 2
    upper = jnp.where(started, pltpu.roll(b, 2, 1) * seed, 0.0)
    lower = jnp.where(started, pltpu.roll(d, 2, 1) * seed, seed)

    fetch_harmonics.wait()
    valid = degree_index < LMAX - order
    even_lane = (lane & 1) == 0
    for r in range(2):
        turned = harmonics[r].T
        real = jnp.where(even_lane, turned, pltpu.roll(turned, 1, 1))
        imag = jnp.where(even_lane, pltpu.roll(turned, SIDE - 1, 1), turned)
        coefficients[2 * r] = jnp.where(valid, real, 0.0)
        coefficients[2 * r + 1] = jnp.where(valid, imag, 0.0)

    def advance(block, state):
        upper, lower, sums = state[0], state[1], list(state[2:])
        for s in range(unroll):
            i = block * unroll + s
            zc = z * first[pl.ds(i, 1), :]
            upper, lower = zc * upper + second[pl.ds(i, 1), :] * lower, upper
            table[i] = upper
            for f in range(4):
                at = 4 * (s % 2) + f
                sums[at] = sums[at] + coefficients[f, pl.ds(i, 1), :] * upper
        return (upper, lower, *sums)

    state = lax.fori_loop(0, SIDE // unroll, advance, (upper, lower) + (zeros,) * 8)
    sums = state[2:]
    high, low = split(jnp.concatenate(sums, axis=0))
    sums = mxu(jnp.concatenate([high, low], axis=1), jnp.concatenate([alike, alike], axis=0))
    small = (2 * ROWS, SIDE)
    pair, lane_half = iota(small, 1) >> 1, iota(small, 1) & 1
    held_sums = jnp.zeros(small, F32)
    for f in range(4):
        both = [sums[(4 * parity + f) * ROWS : (4 * parity + f + 1) * ROWS] for parity in range(2)]
        held_sums = jnp.where(pair == f, jnp.concatenate(both, axis=0), held_sums)
    halves = jnp.concatenate([jnp.where(lane_half == half, held_sums, 0.0) for half in range(2)], axis=0)
    high, low = split(halves)
    own = mxu(jnp.concatenate([picked[...], picked[...]], axis=1), jnp.concatenate([high, low], axis=0))
    even_lane = (iota(square, 1) & 1) == 0
    own = own + jnp.where(even_lane, pltpu.roll(own, SIDE - 1, 1), pltpu.roll(own, 1, 1))
    own = jnp.where(iota(square, 1) < 8, own, 0.0)
    before = pltpu.roll(own, 2, 0)
    after = pltpu.roll(own, 2 * CYCLES - 2, 0)
    sent[...] = own + pltpu.roll(before, 8, 1) + pltpu.roll(after, 16, 1)
    fetch_noise.wait()
    fetch_weights.wait()


def both_halves(pair, b):
    high, low = pair[:, :SIDE], pair[:, SIDE:]
    left = jnp.concatenate([jnp.concatenate([high, high], axis=1), jnp.concatenate([low, low], axis=1)], axis=0)
    product = mxu(left, jnp.concatenate(split(b), axis=0))
    return product[:SIDE] + product[SIDE:]


def row_pairs_swapped(x):
    even = (iota((SIDE, SIDE), 0) & 1) == 0
    return jnp.where(even, pltpu.roll(x, SIDE - 1, 0), pltpu.roll(x, 1, 0))


def euler_kernel(level_weights, turns, basis, basis_turned, small, received, noise, within, across, kappa_out, sent,
                 fields, counts, kappa, gradients, flips, sems):
    cycle = lax.axis_index("ma")
    parity = (cycle + 1 + NPIX // 4 - CYCLES // 2) % 2
    square = (SIDE, SIDE)
    lane, row = iota(square, 1), iota(square, 0)
    real_row = (row & 1) == 0
    a_cos, a_sin = turns[0], turns[1]
    spin_cos, spin_sin, weight = small[0], small[1], small[2]

    arrived = received[...]
    real_lane = ((lane >> 1) & 1) == 0
    partner = jnp.where(real_lane, pltpu.roll(arrived, SIDE - 2, 1), pltpu.roll(arrived, 2, 1))
    turned = (lane < 8) == (parity == 1)
    cs = jnp.where(turned, spin_cos, 1.0)
    sn = jnp.where(turned, spin_sin, 0.0)
    spun = weight * (arrived * cs + jnp.where(real_lane, -partner, partner) * sn)
    lefts = []
    for kk in range(3):
        for r in range(2):
            at = 8 * kk + 4 * r
            real = jnp.broadcast_to(spun[:, at : at + 1], square)
            imag = jnp.broadcast_to(spun[:, at + 2 : at + 3], square)
            lefts.append(jnp.where(real_row, real, -imag) * a_cos - jnp.where(real_row, imag, real) * a_sin)
    maps = both_halves(basis_turned[...], jnp.concatenate(lefts, axis=1))

    def arranged(x, slot):
        flips[slot] = x.T
        return jnp.concatenate([flips[slot, pl.ds(v, 8, stride=16), :] for v in range(16)], axis=0)

    own_noise = arranged(noise[...], 2)
    within_noise, across_noise = arranged(within[...], 3), arranged(across[...], 4)
    second_of_chip = cycle % 2 == 1
    noise_before = jnp.where(second_of_chip, within_noise, across_noise)
    noise_after = jnp.where(second_of_chip, across_noise, within_noise)
    sub = iota((8, SIDE), 0)

    def ratio(kk, r, weights):
        return 2.0 * (maps[:, (2 * kk + r) * SIDE : (2 * kk + r + 1) * SIDE] * weights)

    for r in range(2):
        here = ratio(0, r, own_noise)
        above = jnp.where(cycle > 0, ratio(1, r, noise_before), FAR)
        below = jnp.where(cycle < CYCLES - 1, ratio(2, r, noise_after), FAR)
        for n, x in enumerate((here, below, above)):
            fields[r, n, 8 : 8 + SIDE, :] = x
            last = pltpu.roll(x[SIDE - 8 :], 1, 0)
            fields[r, n, :8, :] = jnp.where(sub == 0, pltpu.roll(last, 1, 1), last)
            first = pltpu.roll(x[:8], 7, 0)
            fields[r, n, 8 + SIDE :, :] = jnp.where(sub == 7, pltpu.roll(first, SIDE - 1, 1), first)
    for r in range(2):
        for v in range(16):
            flips[r, pl.ds(v, 8, stride=16), :] = maps[8 * v : 8 * v + 8, r * SIDE : (r + 1) * SIDE]
        kappa[r] = flips[r].T
    keep_kappa = pltpu.make_async_copy(kappa, kappa_out, sems.at[0])
    keep_kappa.start()

    gradients[...] = jnp.zeros_like(gradients)

    def levels(r, group, odd, top):
        held = range(GROUP)
        number = [group * GROUP + g for g in held]
        twice = [t.astype(F32) * (12.0 / (LEVELS - 1)) - 6.0 for t in number]
        given = [level_weights[r, t] for t in number]
        known = {}

        def soft(n, v):
            if (n, v) not in known:
                x = fields[r, n, 8 * v + 8 : 8 * v + 16, :]
                known[n, v] = [jnp.tanh(x - twice[g]) for g in held]
            return known[n, v]

        totals = [jnp.zeros((8, SIDE), F32)] * GROUP
        for v in range(16):
            ahead, behind = (v + 1, v - 1) if odd else (v - 1, v + 1)
            slope = None
            for g in held:
                u, e, w, d = soft(0, v)[g], soft(0, ahead)[g], soft(0, behind)[g], soft(1, v)[g]
                n1 = -1.0 if top else soft(2, v)[g]
                down = soft(1, ahead)[g] * (d + e)
                up = 1.0 - e if top else soft(2, ahead)[g] * (e + n1)
                inner = down + up + w * (d + n1) - 2.0
                part = inner * (given[g] - (given[g] * u) * u)
                slope = part if slope is None else slope + part
                totals[g] = totals[g] + (u * (2.0 - down - up) if top else u * (2.0 - down))
            gradients[r, 8 * v : 8 * v + 8, :] += slope
        for g in held:
            counts[r * LEVELS + number[g]] = totals[g]

    def sweep(odd, top):
        def step(group, carry):
            for r in range(2):
                levels(r, group, odd, top)
            return carry

        lax.fori_loop(0, LEVELS // GROUP, step, 0)

    pl.when(cycle == 0)(lambda: sweep(True, True))
    pl.when((cycle > 0) & (parity == 1))(lambda: sweep(True, False))
    pl.when(parity == 0)(lambda: sweep(False, False))

    scale = 1.0 / (4.0 * math.sqrt(CYCLES * NPIX))
    back = both_halves(basis[...], jnp.concatenate([gradients[r] * (own_noise * scale) for r in range(2)], axis=1))
    pieces = []
    for r in range(2):
        sums = back[:, r * SIDE : (r + 1) * SIDE]
        pieces += [sums * a_cos, sums * a_sin]
    high, low = split(jnp.concatenate(pieces, axis=1))
    piece, to = iota((4 * SIDE, SIDE), 0) >> 7, iota((4 * SIDE, SIDE), 1)
    gather = (to == (piece >> 1) + 2 * (piece & 1)).astype(BF16)
    near = mxu(high, gather) + mxu(low, gather)
    far = pltpu.roll(row_pairs_swapped(near), SIDE - 2, 1)
    both = near + jnp.where(real_row, -far, far)
    other = row_pairs_swapped(both)
    cs = jnp.where(parity == 1, spin_cos, 1.0)
    sn = jnp.where(parity == 1, spin_sin, 0.0)
    dual = weight * jnp.where(real_row, both * cs - other * sn, -(both * cs + other * sn))
    stacked = jnp.where(lane < 2, dual, 0.0)
    level_sums = jnp.sum(counts[...], axis=1) * -0.125
    level_sums = level_sums + jnp.where(cycle == 0, 2.0 * NPIX / 8.0 / SIDE, 0.0)
    padded = jnp.concatenate([jnp.zeros_like(level_sums), level_sums], axis=0)
    level_row = dot(jnp.ones((8, SIDE), F32), padded, (1, 1))[:1]
    sent[...] = stacked + level_row
    keep_kappa.wait()


def adjoint_kernel(order_rows, received, table, gradient, turned):
    order = order_rows[:1]
    square = (SIDE, SIDE)
    lane, row = iota(square, 1), iota(square, 0)
    arrived = jnp.where(lane < CYCLES, received[...], 0.0)
    real = (row & 1) == 0
    pairs = jnp.where(real, arrived, 0.0) + pltpu.roll(jnp.where(real, 0.0, arrived), 2, 1)
    sel = (4 * ROWS, SIDE)
    at_row = iota(sel, 0)
    odd = (at_row >= 2 * ROWS).astype(jnp.int32)
    at_row = at_row - 2 * ROWS * odd
    in_half = (at_row >= ROWS).astype(jnp.int32)
    pick = selection(iota(sel, 1) >> 1, odd == 1, in_half, at_row - ROWS * in_half).astype(BF16)
    duals = mxu(jnp.concatenate([pick, pick], axis=1), jnp.concatenate(split(pairs), axis=0))
    even = (iota((ROWS, SIDE), 1) & 1) == 0

    def column(parity, half, r, c):
        start = (2 * parity + half) * ROWS
        at = 2 * c + r
        return jnp.broadcast_to(duals[start : start + ROWS, at : at + 1], (ROWS, SIDE))

    factors = [
        [
            (
                jnp.where(even, column(parity, 0, r, 0), column(parity, 1, r, 1)),
                jnp.where(even, column(parity, 0, r, 1), column(parity, 1, r, 0)),
            )
            for r in range(2)
        ]
        for parity in range(2)
    ]

    sub = iota((8, SIDE), 0)

    def merge(a, b, by):
        mine = (sub & by) == 0
        return jnp.where(mine, a, b) + pltpu.roll(jnp.where(mine, b, a), 8 - by, 0)

    even_lane = (iota((8, SIDE), 1) & 1) == 0

    def block(index):
        at = pl.ds(pl.multiple_of(index * 8, 8), 8)
        held = {}
        for s in range(8):
            value = table[index * 8 + s]
            for r in range(2):
                for kind in range(2):
                    product = value * factors[s % 2][r][kind]
                    part = product[:8] + product[8:16] + product[16:]
                    by = 1
                    while s & by:
                        part = merge(held.pop((r, kind, by)), part, by)
                        by *= 2
                    held[r, kind, by] = part
        for r in range(2):
            straight, crossed = held[r, 0, 8], held[r, 1, 8]
            crossed = jnp.where(even_lane, pltpu.roll(crossed, SIDE - 1, 1), pltpu.roll(crossed, 1, 1))
            turned[r, at, :] = straight + crossed

    def blocks(index, carry):
        for more in range(4):
            block(index * 4 + more)
        return carry

    lax.fori_loop(0, SIDE // 8 // 4, blocks, 0)
    for r in range(2):
        degree_index = (row >> 1) * SIDE + lane
        gradient[r] = jnp.where(degree_index < LMAX - order, turned[r].T, 0.0)


VMEM = pl.BlockSpec(memory_space=pltpu.VMEM)
SMEM = pl.BlockSpec(memory_space=pltpu.SMEM)
HBM = pl.BlockSpec(memory_space=pltpu.HBM)
PARAMS = pltpu.CompilerParams(vmem_limit_bytes=40 * 1024 * 1024)


def shards(harmonics, noise_weight, order_table, curve_weight):
    ta_count = lax.axis_size("ta")
    ma_count = lax.axis_size("ma")
    noise = noise_weight.reshape(SIDE, SIDE)
    within = lax.ppermute(noise, "ma", [(i, i ^ 1) for i in range(ma_count)])
    across = lax.ppermute(noise, "ma", [(i, (i + (1 if i % 2 else -1)) % ma_count) for i in range(ma_count)])
    packed = harmonics.reshape(2, 2, 64, SIDE).transpose(0, 2, 1, 3).reshape(2, SIDE, SIDE)
    square = jax.ShapeDtypeStruct((2 * CYCLES, SIDE), F32)
    orders_there = pltpu.with_memory_space_constraint(order_table, pltpu.HBM)
    packed = pltpu.with_memory_space_constraint(packed, pltpu.HBM)
    table, sent, order_rows, turns, basis, basis_turned, small, noise_here, weights = pl.pallas_call(
        legendre_kernel,
        in_specs=[HBM] * 5,
        out_specs=[VMEM] * 9,
        out_shape=[
            jax.ShapeDtypeStruct((SIDE, ROWS, SIDE), F32),
            square,
            jax.ShapeDtypeStruct((8, SIDE), jnp.int32),
            jax.ShapeDtypeStruct((2, SIDE, SIDE), F32),
            jax.ShapeDtypeStruct((SIDE, 2 * SIDE), BF16),
            jax.ShapeDtypeStruct((SIDE, 2 * SIDE), BF16),
            jax.ShapeDtypeStruct((3, SIDE, SIDE), F32),
            jax.ShapeDtypeStruct((SIDE, SIDE), F32),
            jax.ShapeDtypeStruct((2, LEVELS), F32),
        ],
        scratch_shapes=[
            pltpu.VMEM((SIDE, SIDE), F32),
            pltpu.VMEM((SIDE, SIDE), F32),
            pltpu.VMEM((4, SIDE, SIDE), F32),
            pltpu.SMEM((CYCLES,), jnp.int32),
            pltpu.VMEM((2, SIDE, SIDE), F32),
            pltpu.VMEM((1, CYCLES), jnp.int32),
            pltpu.VMEM((2 * CYCLES, 4 * ROWS), BF16),
            pltpu.SemaphoreType.DMA((5,)),
        ],
        compiler_params=PARAMS,
        name="legendre",
    )(
        orders_there,
        pltpu.with_memory_space_constraint(order_table.reshape(1, CYCLES), pltpu.HBM),
        packed,
        pltpu.with_memory_space_constraint(noise, pltpu.HBM),
        pltpu.with_memory_space_constraint(curve_weight, pltpu.HBM),
    )
    sent, within, across = lax.optimization_barrier((sent, within, across))
    received = lax.all_to_all(sent, "ma", split_axis=0, concat_axis=0, tiled=True)
    kappa, sent = pl.pallas_call(
        euler_kernel,
        in_specs=[SMEM] + [VMEM] * 8,
        out_specs=[HBM, VMEM],
        out_shape=[jax.ShapeDtypeStruct((2, SIDE, SIDE), F32), square],
        scratch_shapes=[
            pltpu.VMEM((2, 3, SIDE + 16, SIDE), F32),
            pltpu.VMEM((2 * LEVELS, 8, SIDE), F32),
            pltpu.VMEM((2, SIDE, SIDE), F32),
            pltpu.VMEM((2, SIDE, SIDE), F32),
            pltpu.VMEM((5, SIDE, SIDE), F32),
            pltpu.SemaphoreType.DMA((1,)),
        ],
        compiler_params=PARAMS,
        name="euler",
    )(
        weights,
        turns,
        basis,
        basis_turned,
        small,
        received,
        noise_here,
        within,
        across,
    )
    received = lax.all_to_all(sent, "ma", split_axis=0, concat_axis=0, tiled=True)
    counts = jnp.sum(received.reshape(CYCLES, 2, SIDE)[:, 0, CYCLES:], axis=0).reshape(2, LEVELS)
    one, two, three = [lax.ppermute(counts, "ta", [(i, i ^ by) for i in range(ta_count)]) for by in (1, 2, 3)]
    curve = ((counts + one) + (two + three)) / (ta_count * CYCLES * NPIX)
    gradient = pl.pallas_call(
        adjoint_kernel,
        in_specs=[VMEM, VMEM, VMEM],
        out_specs=VMEM,
        out_shape=jax.ShapeDtypeStruct((2, SIDE, SIDE), F32),
        scratch_shapes=[pltpu.VMEM((2, SIDE, SIDE), F32)],
        compiler_params=PARAMS,
        name="adjoint",
    )(order_rows, received, table)
    gradient = gradient.reshape(2, 64, 2, SIDE).transpose(0, 2, 1, 3).reshape(1, 2, 1, 2, LMAX)
    return kappa.reshape(1, 2, 1, NPIX), curve, gradient


def solution(mesh):
    in_specs = (P("ta", None, "ma", None, None), P("ta", "ma", None), P(), P())
    out_specs = (P("ta", None, "ma", None), P(), P("ta", None, "ma", None, None))
    return jax.shard_map(shards, mesh=mesh, in_specs=in_specs, out_specs=out_specs, check_vma=False)
```

```python
import math

import jax
import jax.numpy as jnp
from jax import lax
from jax.experimental import pallas as pl
from jax.experimental.pallas import tpu as pltpu
from jax.sharding import PartitionSpec as P

F32 = jnp.float32
BF16 = jnp.bfloat16
HIGHEST = lax.Precision.HIGHEST
NPIX = 16384
LMAX = 8192
CYCLES = 64
LEVELS = 32
SIDE = 128
ROWS = 24
GROUP = 4
FAR = -1.0e9


def iota(shape, dim):
    return lax.broadcasted_iota(jnp.int32, shape, dim)


def dot(a, b, contract):
    return lax.dot_general(a, b, ((contract[:1], contract[1:]), ((), ())), precision=HIGHEST,
                           preferred_element_type=F32)


def slot_cycle(half, row):
    own = jnp.where(row < 16, row + 16 * half, -1)
    return jnp.where((row == 16) & (half == 0), 32, own)


def selection(cycle, odd, half, row):
    mirrored = jnp.where(cycle > 32, 64 - cycle, cycle)
    sign = jnp.where((cycle > 32) & odd, -1.0, 1.0)
    return jnp.where(slot_cycle(half, row) == mirrored, sign, 0.0).astype(F32)


def split(x):
    high = x.astype(BF16)
    return high, (x - high.astype(F32)).astype(BF16)


def mxu(a, b):
    return lax.dot_general(a, b, (((1,), (0,)), ((), ())), preferred_element_type=F32)


def turn_cos_sin(index, whole):
    quarter = whole // 4
    index = index & (whole - 1)
    quadrant = (index + quarter // 2) >> (quarter.bit_length() - 1)
    x = (index - quadrant * quarter).astype(F32) * (2.0 * math.pi / whole)
    y = x * x
    sine = x * (1.0 + y * (-1.0 / 6 + y * (1.0 / 120 + y * (-1.0 / 5040 + y * (1.0 / 362880)))))
    cosine = 1.0 + y * (-0.5 + y * (1.0 / 24 + y * (-1.0 / 720 + y * (1.0 / 40320 - y * (1.0 / 3628800)))))
    swap = (quadrant & 1) == 1
    c = jnp.where(swap, sine, cosine)
    s = jnp.where(swap, cosine, sine)
    c = jnp.where(((quadrant + 1) & 2) == 2, -c, c)
    s = jnp.where((quadrant & 2) == 2, -s, s)
    return c, s


def make_basis(orders_row, turns, basis, basis_turned, small):
    square = (SIDE, SIDE)
    lane, row = iota(square, 1), iota(square, 0)
    twice = (iota((CYCLES, SIDE), 1) >> 1) == iota((CYCLES, SIDE), 0)
    eight = jnp.broadcast_to(orders_row[...].astype(F32), (8, CYCLES))
    eight = dot(eight, twice.astype(F32), (1, 0)).astype(jnp.int32)
    orders = jnp.broadcast_to(eight[:1], square)
    down = orders.astype(F32).T.astype(jnp.int32)
    turns[0], turns[1] = turn_cos_sin(down * lane, SIDE)
    pixel = 16 * (row & 7) + (row >> 3)
    cosine, sine = turn_cos_sin(orders * pixel, NPIX)
    turned = jnp.where((lane & 1) == 0, cosine, sine)
    for ref, value in ((basis, turned.T), (basis_turned, turned)):
        ref[:, :SIDE], ref[:, SIDE:] = split(value)
    small[0], small[1] = turn_cos_sin(down, 2 * NPIX)
    small[2] = jnp.where(down == 0, 1.0, 2.0)


def legendre_kernel(orders_in, row_in, harmonics_in, noise_in, weights_in, table, sent, order_out, turns, basis, basis_turned,
                    small_out, noise, weights,
                    first, second, coefficients, orders, harmonics, orders_row, picked, sems):
    ma = lax.axis_index("ma")
    fetch_orders = pltpu.make_async_copy(orders_in, orders, sems.at[0])
    fetch_harmonics = pltpu.make_async_copy(harmonics_in, harmonics, sems.at[1])
    fetch_row = pltpu.make_async_copy(row_in, orders_row, sems.at[2])
    fetch_orders.start()
    fetch_row.start()
    fetch_harmonics.start()
    fetch_noise = pltpu.make_async_copy(noise_in, noise, sems.at[3])
    fetch_weights = pltpu.make_async_copy(weights_in, weights, sems.at[4])
    fetch_noise.start()
    fetch_weights.start()
    square = (SIDE, SIDE)
    alike = ((iota(square, 0) & 1) == (iota(square, 1) & 1)).astype(BF16)
    sel = (2 * CYCLES, 4 * ROWS)
    column = iota(sel, 1)
    in_half = (column >= 2 * ROWS).astype(jnp.int32)
    column = column - 2 * ROWS * in_half
    odd = (column >= ROWS).astype(jnp.int32)
    picked[...] = selection(iota(sel, 0) >> 1, odd == 1, in_half, column - ROWS * odd).astype(BF16)
    shape = (ROWS, SIDE)
    row, half = iota(shape, 0), iota(shape, 1) & 1
    held = slot_cycle(half, row)
    z = jnp.where(held >= 0, 4.0 * (64.0 - 2.0 * held.astype(F32)) / (3.0 * NPIX), 0.0)
    below_one = 1.0 - (1.0 - z * z)
    log_term = -below_one * (1.0 + below_one * (0.5 + below_one * (1.0 / 3.0)))
    fetch_orders.wait()
    order = orders[ma]
    order_out[...] = jnp.full(order_out.shape, order, jnp.int32)
    order_value = order.astype(F32)
    square = (SIDE, SIDE)
    lane, step = iota(square, 1), iota(square, 0)
    degree_index = (lane >> 1) * SIDE + step
    j = degree_index.astype(F32)
    degree = order_value + j
    alpha = jnp.sqrt(
        jnp.maximum((2.0 * degree - 1.0) * (2.0 * degree + 1.0), 0.0)
        / jnp.maximum(j * (j + 2.0 * order_value), 1.0)
    )
    beta = jnp.sqrt(
        jnp.maximum((j - 1.0) * (j - 1.0 + 2.0 * order_value), 0.0)
        / jnp.maximum((2.0 * degree - 3.0) * (2.0 * degree - 1.0), 1.0)
    )
    moving = degree_index > 0
    first[...] = jnp.where(moving, alpha, 0.0)
    second[...] = jnp.where(moving, -alpha * beta, 1.0)
    full = jnp.full(shape, order_value, F32)
    seed = jnp.exp(
        0.5 * jnp.log((2.0 * full + 1.0) / (4.0 * math.pi))
        - 0.25 * jnp.log(math.pi * (full + 0.25))
        + 0.5 * full * log_term
    )

    unroll = 16

    def compose(block, state):
        pu, pl_, qu, ql = state
        for s in range(unroll):
            i = block * unroll + s
            zc = z * first[pl.ds(i, 1), :]
            c2 = second[pl.ds(i, 1), :]
            pu, pl_ = zc * pu + c2 * pl_, pu
            qu, ql = zc * qu + c2 * ql, qu
        return pu, pl_, qu, ql

    fetch_row.wait()
    make_basis(orders_row, turns, basis, basis_turned, small_out)
    ones, zeros = jnp.ones(shape, F32), jnp.zeros(shape, F32)
    a, c, b, d = lax.fori_loop(0, SIDE // unroll, compose, (ones, zeros, zeros, ones))
    lanes = iota(shape, 1)
    for by in (2, 4, 8, 16, 32, 64):
        inside = lanes >= by
        ea = jnp.where(inside, pltpu.roll(a, by, 1), 1.0)
        eb = jnp.where(inside, pltpu.roll(b, by, 1), 0.0)
        ec = jnp.where(inside, pltpu.roll(c, by, 1), 0.0)
        ed = jnp.where(inside, pltpu.roll(d, by, 1), 1.0)
        a, b, c, d = a * ea + b * ec, a * eb + b * ed, c * ea + d * ec, c * eb + d * ed
    started = lanes >= 2
    upper = jnp.where(started, pltpu.roll(b, 2, 1) * seed, 0.0)
    lower = jnp.where(started, pltpu.roll(d, 2, 1) * seed, seed)

    fetch_harmonics.wait()
    valid = degree_index < LMAX - order
    even_lane = (lane & 1) == 0
    for r in range(2):
        turned = harmonics[r].T
        real = jnp.where(even_lane, turned, pltpu.roll(turned, 1, 1))
        imag = jnp.where(even_lane, pltpu.roll(turned, SIDE - 1, 1), turned)
        coefficients[2 * r] = jnp.where(valid, real, 0.0)
        coefficients[2 * r + 1] = jnp.where(valid, imag, 0.0)

    def advance(block, state):
        upper, lower, sums = state[0], state[1], list(state[2:])
        for s in range(unroll):
            i = block * unroll + s
            zc = z * first[pl.ds(i, 1), :]
            upper, lower = zc * upper + second[pl.ds(i, 1), :] * lower, upper
            table[i] = upper
            for f in range(4):
                at = 4 * (s % 2) + f
                sums[at] = sums[at] + coefficients[f, pl.ds(i, 1), :] * upper
        return (upper, lower, *sums)

    state = lax.fori_loop(0, SIDE // unroll, advance, (upper, lower) + (zeros,) * 8)
    sums = state[2:]
    high, low = split(jnp.concatenate(sums, axis=0))
    sums = mxu(jnp.concatenate([high, low], axis=1), jnp.concatenate([alike, alike], axis=0))
    small = (2 * ROWS, SIDE)
    pair, lane_half = iota(small, 1) >> 1, iota(small, 1) & 1
    held_sums = jnp.zeros(small, F32)
    for f in range(4):
        both = [sums[(4 * parity + f) * ROWS : (4 * parity + f + 1) * ROWS] for parity in range(2)]
        held_sums = jnp.where(pair == f, jnp.concatenate(both, axis=0), held_sums)
    halves = jnp.concatenate([jnp.where(lane_half == half, held_sums, 0.0) for half in range(2)], axis=0)
    high, low = split(halves)
    own = mxu(jnp.concatenate([picked[...], picked[...]], axis=1), jnp.concatenate([high, low], axis=0))
    even_lane = (iota(square, 1) & 1) == 0
    own = own + jnp.where(even_lane, pltpu.roll(own, SIDE - 1, 1), pltpu.roll(own, 1, 1))
    own = jnp.where(iota(square, 1) < 8, own, 0.0)
    before = pltpu.roll(own, 2, 0)
    after = pltpu.roll(own, 2 * CYCLES - 2, 0)
    sent[...] = own + pltpu.roll(before, 8, 1) + pltpu.roll(after, 16, 1)
    fetch_noise.wait()
    fetch_weights.wait()


def both_halves(pair, b):
    high, low = pair[:, :SIDE], pair[:, SIDE:]
    left = jnp.concatenate([jnp.concatenate([high, high], axis=1), jnp.concatenate([low, low], axis=1)], axis=0)
    product = mxu(left, jnp.concatenate(split(b), axis=0))
    return product[:SIDE] + product[SIDE:]


def row_pairs_swapped(x):
    even = (iota((SIDE, SIDE), 0) & 1) == 0
    return jnp.where(even, pltpu.roll(x, SIDE - 1, 0), pltpu.roll(x, 1, 0))


def euler_kernel(level_weights, turns, basis, basis_turned, small, received, noise, within, across, kappa_out, sent,
                 fields, counts, kappa, gradients, flips, sems):
    cycle = lax.axis_index("ma")
    parity = (cycle + 1 + NPIX // 4 - CYCLES // 2) % 2
    square = (SIDE, SIDE)
    lane, row = iota(square, 1), iota(square, 0)
    real_row = (row & 1) == 0
    a_cos, a_sin = turns[0], turns[1]
    spin_cos, spin_sin, weight = small[0], small[1], small[2]

    arrived = received[...]
    real_lane = ((lane >> 1) & 1) == 0
    partner = jnp.where(real_lane, pltpu.roll(arrived, SIDE - 2, 1), pltpu.roll(arrived, 2, 1))
    turned = (lane < 8) == (parity == 1)
    cs = jnp.where(turned, spin_cos, 1.0)
    sn = jnp.where(turned, spin_sin, 0.0)
    spun = weight * (arrived * cs + jnp.where(real_lane, -partner, partner) * sn)
    lefts = []
    for kk in range(3):
        for r in range(2):
            at = 8 * kk + 4 * r
            real = jnp.broadcast_to(spun[:, at : at + 1], square)
            imag = jnp.broadcast_to(spun[:, at + 2 : at + 3], square)
            lefts.append(jnp.where(real_row, real, -imag) * a_cos - jnp.where(real_row, imag, real) * a_sin)
    maps = both_halves(basis_turned[...], jnp.concatenate(lefts, axis=1))

    def arranged(x, slot):
        flips[slot] = x.T
        return jnp.concatenate([flips[slot, pl.ds(v, 8, stride=16), :] for v in range(16)], axis=0)

    own_noise = arranged(noise[...], 2)
    within_noise, across_noise = arranged(within[...], 3), arranged(across[...], 4)
    second_of_chip = cycle % 2 == 1
    noise_before = jnp.where(second_of_chip, within_noise, across_noise)
    noise_after = jnp.where(second_of_chip, across_noise, within_noise)
    sub = iota((8, SIDE), 0)

    def ratio(kk, r, weights):
        return 2.0 * (maps[:, (2 * kk + r) * SIDE : (2 * kk + r + 1) * SIDE] * weights)

    for r in range(2):
        here = ratio(0, r, own_noise)
        above = jnp.where(cycle > 0, ratio(1, r, noise_before), FAR)
        below = jnp.where(cycle < CYCLES - 1, ratio(2, r, noise_after), FAR)
        for n, x in enumerate((here, below, above)):
            fields[r, n, 8 : 8 + SIDE, :] = x
            last = pltpu.roll(x[SIDE - 8 :], 1, 0)
            fields[r, n, :8, :] = jnp.where(sub == 0, pltpu.roll(last, 1, 1), last)
            first = pltpu.roll(x[:8], 7, 0)
            fields[r, n, 8 + SIDE :, :] = jnp.where(sub == 7, pltpu.roll(first, SIDE - 1, 1), first)
    for r in range(2):
        for v in range(16):
            flips[r, pl.ds(v, 8, stride=16), :] = maps[8 * v : 8 * v + 8, r * SIDE : (r + 1) * SIDE]
        kappa[r] = flips[r].T
    keep_kappa = pltpu.make_async_copy(kappa, kappa_out, sems.at[0])
    keep_kappa.start()

    gradients[...] = jnp.zeros_like(gradients)

    def levels(r, group, odd, top):
        held = range(GROUP)
        number = [group * GROUP + g for g in held]
        twice = [t.astype(F32) * (12.0 / (LEVELS - 1)) - 6.0 for t in number]
        given = [level_weights[r, t] for t in number]
        known = {}

        def soft(n, v):
            if (n, v) not in known:
                x = fields[r, n, 8 * v + 8 : 8 * v + 16, :]
                known[n, v] = [jnp.tanh(x - twice[g]) for g in held]
            return known[n, v]

        totals = [jnp.zeros((8, SIDE), F32)] * GROUP
        for v in range(16):
            ahead, behind = (v + 1, v - 1) if odd else (v - 1, v + 1)
            slope = None
            for g in held:
                u, e, w, d = soft(0, v)[g], soft(0, ahead)[g], soft(0, behind)[g], soft(1, v)[g]
                n1 = -1.0 if top else soft(2, v)[g]
                down = soft(1, ahead)[g] * (d + e)
                up = 1.0 - e if top else soft(2, ahead)[g] * (e + n1)
                inner = down + up + w * (d + n1) - 2.0
                part = inner * (given[g] - (given[g] * u) * u)
                slope = part if slope is None else slope + part
                totals[g] = totals[g] + (u * (2.0 - down - up) if top else u * (2.0 - down))
            gradients[r, 8 * v : 8 * v + 8, :] += slope
        for g in held:
            counts[r * LEVELS + number[g]] = totals[g]

    def sweep(odd, top):
        def step(group, carry):
            for more in range(2):
                for r in range(2):
                    levels(r, 2 * group + more, odd, top)
            return carry

        lax.fori_loop(0, LEVELS // GROUP // 2, step, 0)

    pl.when(cycle == 0)(lambda: sweep(True, True))
    pl.when((cycle > 0) & (parity == 1))(lambda: sweep(True, False))
    pl.when(parity == 0)(lambda: sweep(False, False))

    scale = 1.0 / (4.0 * math.sqrt(CYCLES * NPIX))
    back = both_halves(basis[...], jnp.concatenate([gradients[r] * (own_noise * scale) for r in range(2)], axis=1))
    pieces = []
    for r in range(2):
        sums = back[:, r * SIDE : (r + 1) * SIDE]
        pieces += [sums * a_cos, sums * a_sin]
    high, low = split(jnp.concatenate(pieces, axis=1))
    piece, to = iota((4 * SIDE, SIDE), 0) >> 7, iota((4 * SIDE, SIDE), 1)
    gather = (to == (piece >> 1) + 2 * (piece & 1)).astype(BF16)
    near = mxu(high, gather) + mxu(low, gather)
    far = pltpu.roll(row_pairs_swapped(near), SIDE - 2, 1)
    both = near + jnp.where(real_row, -far, far)
    other = row_pairs_swapped(both)
    cs = jnp.where(parity == 1, spin_cos, 1.0)
    sn = jnp.where(parity == 1, spin_sin, 0.0)
    dual = weight * jnp.where(real_row, both * cs - other * sn, -(both * cs + other * sn))
    stacked = jnp.where(lane < 2, dual, 0.0)
    level_sums = jnp.sum(counts[...], axis=1) * -0.125
    level_sums = level_sums + jnp.where(cycle == 0, 2.0 * NPIX / 8.0 / SIDE, 0.0)
    padded = jnp.concatenate([jnp.zeros_like(level_sums), level_sums], axis=0)
    level_row = dot(jnp.ones((8, SIDE), F32), padded, (1, 1))[:1]
    sent[...] = stacked + level_row
    keep_kappa.wait()


def adjoint_kernel(order_rows, received, table, gradient, turned):
    order = order_rows[:1]
    square = (SIDE, SIDE)
    lane, row = iota(square, 1), iota(square, 0)
    arrived = jnp.where(lane < CYCLES, received[...], 0.0)
    real = (row & 1) == 0
    pairs = jnp.where(real, arrived, 0.0) + pltpu.roll(jnp.where(real, 0.0, arrived), 2, 1)
    sel = (4 * ROWS, SIDE)
    at_row = iota(sel, 0)
    odd = (at_row >= 2 * ROWS).astype(jnp.int32)
    at_row = at_row - 2 * ROWS * odd
    in_half = (at_row >= ROWS).astype(jnp.int32)
    pick = selection(iota(sel, 1) >> 1, odd == 1, in_half, at_row - ROWS * in_half).astype(BF16)
    duals = mxu(jnp.concatenate([pick, pick], axis=1), jnp.concatenate(split(pairs), axis=0))
    even = (iota((ROWS, SIDE), 1) & 1) == 0

    def column(parity, half, r, c):
        start = (2 * parity + half) * ROWS
        at = 2 * c + r
        return jnp.broadcast_to(duals[start : start + ROWS, at : at + 1], (ROWS, SIDE))

    factors = [
        [
            (
                jnp.where(even, column(parity, 0, r, 0), column(parity, 1, r, 1)),
                jnp.where(even, column(parity, 0, r, 1), column(parity, 1, r, 0)),
            )
            for r in range(2)
        ]
        for parity in range(2)
    ]

    sub = iota((8, SIDE), 0)

    def merge(a, b, by):
        mine = (sub & by) == 0
        return jnp.where(mine, a, b) + pltpu.roll(jnp.where(mine, b, a), 8 - by, 0)

    even_lane = (iota((8, SIDE), 1) & 1) == 0

    def block(index):
        at = pl.ds(pl.multiple_of(index * 8, 8), 8)
        held = {}
        for s in range(8):
            value = table[index * 8 + s]
            for r in range(2):
                for kind in range(2):
                    product = value * factors[s % 2][r][kind]
                    part = product[:8] + product[8:16] + product[16:]
                    by = 1
                    while s & by:
                        part = merge(held.pop((r, kind, by)), part, by)
                        by *= 2
                    held[r, kind, by] = part
        for r in range(2):
            straight, crossed = held[r, 0, 8], held[r, 1, 8]
            crossed = jnp.where(even_lane, pltpu.roll(crossed, SIDE - 1, 1), pltpu.roll(crossed, 1, 1))
            turned[r, at, :] = straight + crossed

    def blocks(index, carry):
        for more in range(4):
            block(index * 4 + more)
        return carry

    lax.fori_loop(0, SIDE // 8 // 4, blocks, 0)
    for r in range(2):
        degree_index = (row >> 1) * SIDE + lane
        gradient[r] = jnp.where(degree_index < LMAX - order, turned[r].T, 0.0)


VMEM = pl.BlockSpec(memory_space=pltpu.VMEM)
SMEM = pl.BlockSpec(memory_space=pltpu.SMEM)
HBM = pl.BlockSpec(memory_space=pltpu.HBM)
PARAMS = pltpu.CompilerParams(vmem_limit_bytes=40 * 1024 * 1024)


def shards(harmonics, noise_weight, order_table, curve_weight):
    ta_count = lax.axis_size("ta")
    ma_count = lax.axis_size("ma")
    noise = noise_weight.reshape(SIDE, SIDE)
    within = lax.ppermute(noise, "ma", [(i, i ^ 1) for i in range(ma_count)])
    across = lax.ppermute(noise, "ma", [(i, (i + (1 if i % 2 else -1)) % ma_count) for i in range(ma_count)])
    packed = harmonics.reshape(2, 2, 64, SIDE).transpose(0, 2, 1, 3).reshape(2, SIDE, SIDE)
    square = jax.ShapeDtypeStruct((2 * CYCLES, SIDE), F32)
    orders_there = pltpu.with_memory_space_constraint(order_table, pltpu.HBM)
    packed = pltpu.with_memory_space_constraint(packed, pltpu.HBM)
    table, sent, order_rows, turns, basis, basis_turned, small, noise_here, weights = pl.pallas_call(
        legendre_kernel,
        in_specs=[HBM] * 5,
        out_specs=[VMEM] * 9,
        out_shape=[
            jax.ShapeDtypeStruct((SIDE, ROWS, SIDE), F32),
            square,
            jax.ShapeDtypeStruct((8, SIDE), jnp.int32),
            jax.ShapeDtypeStruct((2, SIDE, SIDE), F32),
            jax.ShapeDtypeStruct((SIDE, 2 * SIDE), BF16),
            jax.ShapeDtypeStruct((SIDE, 2 * SIDE), BF16),
            jax.ShapeDtypeStruct((3, SIDE, SIDE), F32),
            jax.ShapeDtypeStruct((SIDE, SIDE), F32),
            jax.ShapeDtypeStruct((2, LEVELS), F32),
        ],
        scratch_shapes=[
            pltpu.VMEM((SIDE, SIDE), F32),
            pltpu.VMEM((SIDE, SIDE), F32),
            pltpu.VMEM((4, SIDE, SIDE), F32),
            pltpu.SMEM((CYCLES,), jnp.int32),
            pltpu.VMEM((2, SIDE, SIDE), F32),
            pltpu.VMEM((1, CYCLES), jnp.int32),
            pltpu.VMEM((2 * CYCLES, 4 * ROWS), BF16),
            pltpu.SemaphoreType.DMA((5,)),
        ],
        compiler_params=PARAMS,
        name="legendre",
    )(
        orders_there,
        pltpu.with_memory_space_constraint(order_table.reshape(1, CYCLES), pltpu.HBM),
        packed,
        pltpu.with_memory_space_constraint(noise, pltpu.HBM),
        pltpu.with_memory_space_constraint(curve_weight, pltpu.HBM),
    )
    sent, within, across = lax.optimization_barrier((sent, within, across))
    received = lax.all_to_all(sent, "ma", split_axis=0, concat_axis=0, tiled=True)
    kappa, sent = pl.pallas_call(
        euler_kernel,
        in_specs=[SMEM] + [VMEM] * 8,
        out_specs=[HBM, VMEM],
        out_shape=[jax.ShapeDtypeStruct((2, SIDE, SIDE), F32), square],
        scratch_shapes=[
            pltpu.VMEM((2, 3, SIDE + 16, SIDE), F32),
            pltpu.VMEM((2 * LEVELS, 8, SIDE), F32),
            pltpu.VMEM((2, SIDE, SIDE), F32),
            pltpu.VMEM((2, SIDE, SIDE), F32),
            pltpu.VMEM((5, SIDE, SIDE), F32),
            pltpu.SemaphoreType.DMA((1,)),
        ],
        compiler_params=PARAMS,
        name="euler",
    )(
        weights,
        turns,
        basis,
        basis_turned,
        small,
        received,
        noise_here,
        within,
        across,
    )
    received = lax.all_to_all(sent, "ma", split_axis=0, concat_axis=0, tiled=True)
    counts = jnp.sum(received.reshape(CYCLES, 2, SIDE)[:, 0, CYCLES:], axis=0).reshape(2, LEVELS)
    one, two, three = [lax.ppermute(counts, "ta", [(i, i ^ by) for i in range(ta_count)]) for by in (1, 2, 3)]
    curve = ((counts + one) + (two + three)) / (ta_count * CYCLES * NPIX)
    gradient = pl.pallas_call(
        adjoint_kernel,
        in_specs=[VMEM, VMEM, VMEM],
        out_specs=VMEM,
        out_shape=jax.ShapeDtypeStruct((2, SIDE, SIDE), F32),
        scratch_shapes=[pltpu.VMEM((2, SIDE, SIDE), F32)],
        compiler_params=PARAMS,
        name="adjoint",
    )(order_rows, received, table)
    gradient = gradient.reshape(2, 64, 2, SIDE).transpose(0, 2, 1, 3).reshape(1, 2, 1, 2, LMAX)
    return kappa.reshape(1, 2, 1, NPIX), curve, gradient


def solution(mesh):
    in_specs = (P("ta", None, "ma", None, None), P("ta", "ma", None), P(), P())
    out_specs = (P("ta", None, "ma", None), P(), P("ta", None, "ma", None, None))
    return jax.shard_map(shards, mesh=mesh, in_specs=in_specs, out_specs=out_specs, check_vma=False)
```
